256 devices in a mesh: space: 64 (over z, x, core), inst: 4 (over y).
Axes of the slice: x: 4, y: 4, z: 8, core: 2. Of those that a mesh axis runs over, the one named last changes fastest.
Arguments:
- basis_rows: bfloat16 [2, 196608, 512], P(None, 'space'), may hold values from -0.75 to 0.75
- reference_state: float32 [2, 196608], P(None, 'space'), may hold values from -3 to 3
- burning: int32 [196608], P('space'), may hold values 0 or 1
- coords_now: float32 [4, 512], P('inst'), may hold values from -1.5 to 1.5
- coords_before: float32 [4, 512], P('inst'), may hold values from -1.5 to 1.5
- diffusivity: float32 [4], P('inst'), may hold values from 0.5 to 2
- advection: float32 [4], P('inst'), may hold values from 0.5 to 1.5
- reaction_rate: float32 [4], P('inst'), may hold values from 0.2 to 1
Outputs:
- jacobian: bfloat16 [4, 2, 196608, 512], P('inst', None, 'space')
- residual: float32 [4, 2, 196608], P('inst', None, 'space')
- update: float32 [4, 512], P('inst')
The draws below stay inside these ranges and needn't reach their ends.
All inputs are finite; a program needn't handle non-finite values. No bound on the sum of `burning` on one device may be relied on, other than what follows from the above.
Results may differ from the reference program's by a relative error of at most 0.0034.
Values may be sent and summed in bfloat16 or wider, within the bound.
No kernel may reach another device: no remote copies, remote signals or barrier semaphores. Data moves between devices by JAX's collectives and lax.ppermute only.
A program may use at most 128 MiB of HBM per device.

```python
import math
import jax
import jax.numpy as jnp
from jax import lax

MODES = 512
CELLS_DEV = 3072
INST = 4
CELLS = 196608
N_SPACE = 64


def draw_basis_rows(key, part):
    key = jax.random.fold_in(key, 11)
    partner_one = jax.random.permutation(jax.random.fold_in(key, 1), MODES)
    partner_two = jax.random.permutation(jax.random.fold_in(key, 2), MODES)
    partner_three = jax.random.permutation(jax.random.fold_in(key, 3), MODES)
    weights = jax.random.uniform(jax.random.fold_in(key, 5), (3, MODES), jnp.float32, 0.25, 0.32)
    mode_scale = jnp.exp(jax.random.uniform(jax.random.fold_in(key, 6), (MODES,), jnp.float32, math.log(0.5), math.log(1.5)))

    def one_variable(index):
        subkey = jax.random.fold_in(key, 100 + index)
        fields = 0.1 * jnp.clip(jax.random.normal(subkey, (CELLS, MODES), jnp.float32), -2.5, 2.5)
        mixed = fields + weights[0] * jnp.take(fields, partner_one, axis=1)
        mixed = mixed + weights[1] * jnp.take(fields, partner_two, axis=1)
        mixed = mixed + weights[2] * jnp.take(fields, partner_three, axis=1)
        return (mixed * mode_scale).astype(jnp.bfloat16)
    return lax.map(one_variable, jnp.arange(2, dtype=jnp.int32))


def with_ends(drawn, stream_key, low, largest):
    shape = drawn.shape
    spot = [jax.random.randint(jax.random.fold_in(stream_key, axis), (), 0, shape[axis]) for axis in range(len(shape))]
    drawn = drawn.at[tuple(spot)].set(low)
    longest = shape.index(max(shape))
    spot[longest] = (spot[longest] + 1) % shape[longest]
    return drawn.at[tuple(spot)].set(largest)


def steps_of(rng, dims, shards, smallest, top_value):
    factor_of, own = 1.0, jax.random.fold_in(rng, 6)
    for dim, shards_of in shards:
        draws = jnp.exp(jax.random.uniform(jax.random.fold_in(own, dim), (shards_of,), jnp.float32, smallest / len(shards), top_value / len(shards)))
        factor_of = factor_of * jnp.repeat(draws, dims[dim] // shards_of).reshape([-1 if axis == dim else 1 for axis in range(len(dims))])
    return factor_of


def normal_values(own_key, extent, deviation, most, pieces=(), kind=jnp.bfloat16):
    loudness = steps_of(own_key, extent, pieces, -0.22, 0.18) if pieces else 1.0
    result = jax.random.normal(own_key, extent, jnp.float32) * deviation * loudness
    return jnp.minimum(jnp.maximum(result, -most), most).astype(kind)


def setup_inputs(seed: int = 0) -> dict:
    key_list = jax.random.split(jax.random.key(seed), 9)
    basis_rows = draw_basis_rows(jax.random.fold_in(key_list[8], 71), 0)
    reference_state = normal_values(key_list[1], (2, CELLS), 0.5, 3.0, ((1, 64),), jnp.float32)
    burning = with_ends((jax.random.randint(key_list[2], (CELLS,), 0, 2) < 1).astype(jnp.int32), jax.random.fold_in(key_list[2], 1), 0, 1)
    coords_now = normal_values(key_list[3], (INST, MODES), 0.25, 1.5, ((0, 4),), jnp.float32)
    coords_before = normal_values(key_list[4], (INST, MODES), 0.25, 1.5, ((0, 4),), jnp.float32)
    diffusivity = jnp.clip(jnp.exp(math.log(2.0) - 1.3862944 * jax.random.uniform(key_list[5], (INST,), jnp.float32) ** steps_of(key_list[5], (INST,), ((0, 4),), -0.2, 0.2)), 0.5, 2.0)
    advection = jnp.clip(0.5 + 1.0 * jax.random.uniform(key_list[6], (INST,), jnp.float32) ** steps_of(key_list[6], (INST,), ((0, 4),), -0.2, 0.2), 0.5, 1.5)
    reaction_rate = jnp.clip(jnp.exp(math.log(1.0) - 1.609438 * jax.random.uniform(key_list[7], (INST,), jnp.float32) ** steps_of(key_list[7], (INST,), ((0, 4),), -0.2, 0.2)), 0.2, 1.0)
    return dict(basis_rows=basis_rows, reference_state=reference_state, burning=burning, coords_now=coords_now, coords_before=coords_before, diffusivity=diffusivity, advection=advection, reaction_rate=reaction_rate)


time_step = 0.5

def operate(padded, diffuse, advect):
    centre = padded[:, 1:-1]
    left_side = padded[:, :-2]
    right_side = padded[:, 2:]
    return diffuse * (left_side - 2.0 * centre + right_side) - advect * (centre - left_side)

def jacobian_rows(basis_piece, fuel_slope, heat_slope, diffuse, advect):
    widened = basis_piece.astype(jnp.float32)
    centre = widened[:, 1:-1]
    transport = operate(widened, diffuse, advect)
    fuel_col = centre[0] - time_step * (transport[0] - fuel_slope[:, None] * centre[0] - heat_slope[:, None] * centre[1])
    heat_col = centre[1] - time_step * (transport[1] + fuel_slope[:, None] * centre[0] + heat_slope[:, None] * centre[1])
    return jnp.stack([fuel_col, heat_col]).astype(jnp.bfloat16)

def solve_update(system, right_hand):
    factor_low = jnp.linalg.cholesky(system)
    half_solved = lax.linalg.triangular_solve(factor_low, right_hand[:, None], left_side=True, lower=True)
    solved = lax.linalg.triangular_solve(factor_low, half_solved, left_side=True, lower=True, transpose_a=True)
    return -solved[:, 0]

def one_instance(basis_rows, reference_state, burning, coords_now, coords_before, diffuse, advect, rate):
    cell_total = basis_rows.shape[1]
    mode_total = basis_rows.shape[2]
    matrix = basis_rows.reshape(2 * cell_total, mode_total)
    state_now = reference_state + jnp.dot(matrix.astype(jnp.float32), coords_now.astype(jnp.bfloat16).astype(jnp.float32), preferred_element_type=jnp.float32).reshape(2, cell_total)
    change = jnp.dot(matrix.astype(jnp.float32), (coords_now - coords_before).astype(jnp.bfloat16).astype(jnp.float32), preferred_element_type=jnp.float32).reshape(2, cell_total)
    padded_state = jnp.pad(state_now, ((0, 0), (1, 1)))
    flux_sum = operate(padded_state, diffuse, advect)
    fuel_part = state_now[0]
    heat_part = state_now[1]
    active = burning.astype(jnp.float32)
    tangent = jnp.tanh(heat_part)
    reaction = rate * active * fuel_part * (1.0 + tangent)
    residual = change - time_step * (flux_sum + jnp.stack([-reaction, reaction]))
    fuel_slope = rate * active * (1.0 + tangent)
    heat_slope = rate * active * fuel_part * (1.0 - tangent * tangent)
    padded_basis = jnp.pad(basis_rows, ((0, 0), (1, 1), (0, 0)))

    def block_rows(block_id):
        start = (block_id * CELLS_DEV).astype(jnp.int32)
        basis_piece = lax.dynamic_slice_in_dim(padded_basis, start, CELLS_DEV + 2, 1)
        fuel_block = lax.dynamic_slice_in_dim(fuel_slope, start, CELLS_DEV, 0)
        heat_block = lax.dynamic_slice_in_dim(heat_slope, start, CELLS_DEV, 0)
        return jacobian_rows(basis_piece, fuel_block, heat_block, diffuse, advect)
    stacked = lax.map(block_rows, jnp.arange(N_SPACE, dtype=jnp.int32))
    jacobian = stacked.transpose(1, 0, 2, 3).reshape(2, cell_total, mode_total)
    flat_jac = jacobian.reshape(2 * cell_total, mode_total)
    system = lax.dot_general(flat_jac.astype(jnp.float32), flat_jac.astype(jnp.float32), (((0,), (0,)), ((), ())), preferred_element_type=jnp.float32)
    right_hand = lax.dot_general(flat_jac.astype(jnp.float32), residual.astype(jnp.bfloat16).reshape(2 * cell_total).astype(jnp.float32), (((0,), (0,)), ((), ())), preferred_element_type=jnp.float32)
    return (jacobian, residual, solve_update(system, right_hand))

def reference(basis_rows, reference_state, burning, coords_now, coords_before, diffusivity, advection, reaction_rate):
    jac_list = []
    res_list = []
    upd_list = []
    for instance in range(INST):
        jacobian, residual, update = one_instance(basis_rows, reference_state, burning, coords_now[instance], coords_before[instance], diffusivity[instance], advection[instance], reaction_rate[instance])
        jac_list.append(jacobian)
        res_list.append(residual)
        upd_list.append(update)
    return (jnp.stack(jac_list), jnp.stack(res_list), jnp.stack(upd_list))
```

```python
import functools

import jax
import jax.numpy as jnp
from jax import lax
from jax.experimental import pallas as pl
from jax.experimental.pallas import tpu as pltpu
from jax.sharding import Mesh
from jax.sharding import PartitionSpec as P

PLANE = ("space_0", "space_1")
CORE = "space_2"
SPACE = (*PLANE, CORE)
F32 = jnp.float32
BF16 = jnp.bfloat16

time_step = 0.5
LANE = 128
STEP_CELLS = 512
EXACT = lax.Precision.HIGHEST


def dot_rows(a, b):
    return lax.dot_general(a, b, (((1,), (1,)), ((), ())), preferred_element_type=F32)


def dot_columns(a, b):
    return lax.dot_general(a, b, (((0,), (0,)), ((), ())), preferred_element_type=F32)


def tile_pairs(count):
    return [(i, j) for i in range(count) for j in range(i, count)]


def rows_kernel(
    core_ref, nu_ref, adv_ref, rate_ref, basis_ref, before_ref, after_ref, halo_low_ref, halo_high_ref,
    ref_ref, burn_ref, now_ref, old_ref, jac_ref, res_ref, own_ref, other_ref, acc, right, *, steps, size
):
    step = pl.program_id(0)
    modes = basis_ref.shape[2]
    nu, adv, rate = nu_ref[0], adv_ref[0], rate_ref[0]
    now = now_ref[...].astype(BF16)
    diff = (now_ref[...] - old_ref[...]).astype(BF16)
    now32 = now.astype(F32)
    coords = jnp.concatenate([now, diff, jnp.zeros((6, modes), BF16)], axis=0)
    first, last = step == 0, step == steps - 1
    start = pl.multiple_of(step * size, size)
    lanes = lax.broadcasted_iota(jnp.int32, (1, size), 1)
    edge, state, moved, flux = [], [], [], []
    for v in range(2):
        low = jnp.where(first, halo_low_ref[v : v + 1, :modes], before_ref[v, 15:16, :].astype(F32))
        high = jnp.where(last, halo_high_ref[v : v + 1, :modes], after_ref[v, 0:1, :].astype(F32))
        edge.append((low, high))
        both = dot_rows(coords, basis_ref[v])
        here = ref_ref[v : v + 1, pl.ds(start, size)] + both[0:1]
        below = pl.multiple_of(jnp.maximum(start - LANE, 0), LANE)
        above = pl.multiple_of(jnp.minimum(start + size, (steps - 1) * size), LANE)
        ref_low = ref_ref[v : v + 1, pl.ds(below, LANE)][:, LANE - 1 : LANE]
        ref_high = ref_ref[v : v + 1, pl.ds(above, LANE)][:, 0:1]
        ref_low = jnp.where(first, halo_low_ref[v : v + 1, modes : modes + 1], ref_low)
        ref_high = jnp.where(last, halo_high_ref[v : v + 1, modes : modes + 1], ref_high)
        state_low = ref_low + jnp.sum(low * now32, axis=1, keepdims=True)
        state_high = ref_high + jnp.sum(high * now32, axis=1, keepdims=True)
        left = jnp.where(lanes == 0, state_low, pltpu.roll(here, 1, 1))
        following = jnp.where(lanes == size - 1, state_high, pltpu.roll(here, size - 1, 1))
        flux.append(nu * (left - 2.0 * here + following) - adv * (here - left))
        state.append(here)
        moved.append(both[1:2])
    active = burn_ref[0:1, pl.ds(start, size)].astype(F32)
    tangent = jnp.tanh(state[1])
    a = rate * active * (1.0 + tangent)
    w = a * state[0]
    e = rate * active * state[0] * (1.0 - tangent * tangent)
    res = [moved[0] - time_step * (flux[0] - w), moved[1] - time_step * (flux[1] + w)]
    res_ref[0:1, :] = res[0]
    res_ref[1:2, :] = res[1]
    mid = 1.0 + time_step * (2.0 * nu + adv)
    lower = time_step * (nu + adv)
    upper = time_step * nu
    rows = lax.broadcasted_iota(jnp.int32, (LANE, modes), 0)
    for t in range(size // LANE):
        lo = LANE * t
        a_col = jnp.broadcast_to(time_step * a[:, lo : lo + LANE], (LANE, LANE)).T
        e_col = jnp.broadcast_to(time_step * e[:, lo : lo + LANE], (LANE, LANE)).T
        a_col = jnp.concatenate([a_col] * (modes // LANE), axis=1)
        e_col = jnp.concatenate([e_col] * (modes // LANE), axis=1)
        parts, mids = [], []
        for v in range(2):
            x = basis_ref[v, lo : lo + LANE, :].astype(F32)
            low = edge[v][0] if t == 0 else basis_ref[v, lo - 16 : lo, :].astype(F32)[15:16]
            end = lo + LANE
            high = edge[v][1] if end == size else basis_ref[v, end : end + 16, :].astype(F32)[0:1]
            left = jnp.where(rows == 0, low, pltpu.roll(x, 1, 0))
            following = jnp.where(rows == LANE - 1, high, pltpu.roll(x, LANE - 1, 0))
            parts.append(mid * x - lower * left - upper * following)
            mids.append(x)
        source = a_col * mids[0] + e_col * mids[1]
        jac_ref[0, lo : lo + LANE, :] = (parts[0] + source).astype(BF16)
        jac_ref[1, lo : lo + LANE, :] = (parts[1] - source).astype(BF16)
    j0, j1 = jac_ref[0], jac_ref[1]
    r = jnp.dot(jnp.broadcast_to(res[0].astype(BF16), (8, size)), j0, preferred_element_type=F32)
    r += jnp.dot(jnp.broadcast_to(res[1].astype(BF16), (8, size)), j1, preferred_element_type=F32)
    half = modes // 2
    top = dot_columns(j0[:, :half], j0) + dot_columns(j1[:, :half], j1)
    bottom = dot_columns(j0[:, half:], j0[:, half:]) + dot_columns(j1[:, half:], j1[:, half:])

    @pl.when(first)
    def _():
        acc[0:half, :] = top
        acc[half:, half:] = bottom
        right[...] = r

    @pl.when(jnp.logical_not(first))
    def _():
        acc[0:half, :] += top
        acc[half:, half:] += bottom
        right[...] += r

    def write(target, which):
        pairs = tile_pairs(modes // LANE)
        rows_half = target.shape[0]
        base = which * rows_half
        for t, (i, j) in enumerate(pairs):
            at = LANE * t - base
            if 0 <= at < rows_half:
                target[at : at + LANE, :] = acc[LANE * i : LANE * i + LANE, LANE * j : LANE * j + LANE]
        at = LANE * len(pairs) - base
        if 0 <= at < rows_half:
            target[at:, :] = jnp.zeros((rows_half - at, LANE), F32)
            for i in range(modes // LANE):
                target[at + 8 * i : at + 8 * i + 1, :] = right[0:1, LANE * i : LANE * i + LANE]

    for core in range(2):

        @pl.when(last & (core_ref[0] == core))
        def _():
            write(own_ref, core)
            write(other_ref, 1 - core)


def packed_rows(modes):
    count = modes // LANE
    return -(-(LANE * len(tile_pairs(count)) + 8 * count) // 512) * 512


def rows_and_sums(core, nu, adv, rate, basis, halo_low, halo_high, ref, burn, now, old):
    cells, modes = basis.shape[1:]
    size = STEP_CELLS
    steps = cells // size
    per = size // 16
    smem = pl.BlockSpec(memory_space=pltpu.SMEM)
    half = packed_rows(modes) // 2

    def whole(shape):
        return pl.BlockSpec(shape, lambda i: (0,) * len(shape))

    return pl.pallas_call(
        functools.partial(rows_kernel, steps=steps, size=size),
        grid=(steps,),
        in_specs=[
            smem, smem, smem, smem,
            pl.BlockSpec((2, size, modes), lambda i: (0, i, 0)),
            pl.BlockSpec((2, 16, modes), lambda i: (0, jnp.maximum(i * per - 1, 0), 0)),
            pl.BlockSpec((2, 16, modes), lambda i: (0, jnp.minimum(i * per + per, cells // 16 - 1), 0)),
            whole(halo_low.shape), whole(halo_high.shape), whole(ref.shape), whole(burn.shape),
            whole(now.shape), whole(old.shape),
        ],
        out_specs=[
            pl.BlockSpec((2, size, modes), lambda i: (0, i, 0)),
            pl.BlockSpec((2, size), lambda i: (0, i)),
            whole((half, LANE)),
            whole((half, LANE)),
        ],
        out_shape=[
            jax.ShapeDtypeStruct((2, cells, modes), BF16),
            jax.ShapeDtypeStruct((2, cells), F32),
            jax.ShapeDtypeStruct((half, LANE), F32),
            jax.ShapeDtypeStruct((half, LANE), F32),
        ],
        scratch_shapes=[pltpu.VMEM((modes, modes), F32), pltpu.VMEM((8, modes), F32)],
        compiler_params=pltpu.CompilerParams(vmem_limit_bytes=48 * 2**20),
    )(core, nu, adv, rate, basis, basis, basis, halo_low, halo_high, ref, burn, now, old)


def reciprocal(x):
    y = pltpu.reciprocal(x, approx=True)
    y = y * (2.0 - x * y)
    return y * (2.0 - x * y)


def inverse_block(block):
    width = block.shape[1]
    groups = [block[8 * g : 8 * g + 8] for g in range(width // 8)]
    full = (8, width)
    lanes = lax.broadcasted_iota(jnp.int32, full, 1)
    subs = lax.broadcasted_iota(jnp.int32, full, 0)
    for p in range(len(groups)):
        panel = groups[p]
        base = 8 * p
        cols = [jnp.broadcast_to(panel[:, base + j : base + j + 1], full) for j in range(8)]
        entry = [[jnp.broadcast_to(cols[t][s : s + 1], full) if t >= s else None for t in range(8)] for s in range(8)]
        window = (lanes >= base) & (lanes < base + 8)
        opened = jnp.where(window, jnp.where(lanes == subs + base, 1.0, 0.0), panel)
        rows = [jnp.broadcast_to(opened[s : s + 1], full) for s in range(8)]
        inv = []
        for j in range(8):
            inv.append(reciprocal(entry[j][j]))
            for s in [*range(j + 1, 8), *range(j)]:
                mult = (entry[j][s] if s > j else entry[s][j]) * inv[j]
                for t in range(max(s, j + 1), 8):
                    entry[s][t] = entry[s][t] - mult * entry[j][t]
                rows[s] = rows[s] - mult * rows[j]
        rows = [rows[s] * inv[s] for s in range(8)]
        for g in range(len(groups)):
            if g == p:
                continue
            terms = [jnp.broadcast_to(groups[g][:, base + s : base + s + 1], full) * rows[s] for s in range(8)]
            while len(terms) > 1:
                terms = [a + b for a, b in zip(terms[::2], terms[1::2])]
            groups[g] = jnp.where(window, 0.0, groups[g]) - terms[0]
        whole = rows[0]
        for s in range(1, 8):
            whole = jnp.where(subs == s, rows[s], whole)
        groups[p] = whole
    return jnp.concatenate(groups, axis=0)


def exact_dot(a, b, dims=((1,), (0,))):
    return lax.dot_general(a, b, (dims, ((), ())), precision=EXACT, preferred_element_type=F32)


def solve_kernel(core_ref, own_ref, other_ref, out_ref, packed, work, panel, *, count):
    half = own_ref.shape[0]
    core = core_ref[0]
    packed[pl.ds(pl.multiple_of(core * half, half), half), :] = own_ref[...]
    packed[pl.ds(pl.multiple_of((1 - core) * half, half), half), :] = other_ref[...]
    modes = count * LANE
    pairs = tile_pairs(count)
    for t, (i, j) in enumerate(pairs):
        work[LANE * i : LANE * i + LANE, LANE * j : LANE * j + LANE] = packed[LANE * t : LANE * t + LANE, :]
    for i in range(count):
        at = LANE * len(pairs) + 8 * i
        r = jnp.broadcast_to(packed[at : at + 1, :], (LANE, LANE))
        work[LANE * i : LANE * i + LANE, modes : modes + LANE] = r.T
    for k in range(count):
        lo = LANE * k
        end = lo + LANE
        x = exact_dot(inverse_block(work[lo:end, lo:end]), work[lo:end, end:])
        panel[lo:end, end:] = x
        for i in range(k + 1, count):
            a = LANE * i
            work[a : a + LANE, a:] -= exact_dot(work[lo:end, a : a + LANE], x[:, a - end :], ((0,), (0,)))
    solved = {}
    for k in reversed(range(count)):
        lo = LANE * k
        u = panel[lo : lo + LANE, modes:]
        for i in range(k + 1, count):
            u = u - exact_dot(panel[lo : lo + LANE, LANE * i : LANE * i + LANE], solved[i])
        solved[k] = u
        out_ref[0:1, lo : lo + LANE] = -u.T[0:1]


def solve_update(core, own, other, modes):
    vmem = pl.BlockSpec(memory_space=pltpu.VMEM)
    return pl.pallas_call(
        functools.partial(solve_kernel, count=modes // LANE),
        out_shape=jax.ShapeDtypeStruct((1, modes), F32),
        in_specs=[pl.BlockSpec(memory_space=pltpu.SMEM), vmem, vmem],
        out_specs=vmem,
        scratch_shapes=[
            pltpu.VMEM((2 * own.shape[0], LANE), F32),
            pltpu.VMEM((modes, modes + LANE), F32),
            pltpu.VMEM((modes, modes + LANE), F32),
        ],
        compiler_params=pltpu.CompilerParams(vmem_limit_bytes=48 * 2**20),
    )(core, own, other)


def swapped(shard):
    return lax.ppermute(shard, CORE, [(0, 1), (1, 0)])


def summed_over_plane(shard):
    count = lax.axis_size(PLANE)
    blocks = shard.reshape(count, shard.shape[0] // count, shard.shape[1])
    mine = jnp.sum(lax.all_to_all(blocks, PLANE, 0, 0, tiled=True), axis=0)
    copies = jnp.broadcast_to(mine, blocks.shape)
    return lax.all_to_all(copies, PLANE, 0, 0, tiled=True).reshape(shard.shape)


def edge_message(basis_row, state_value):
    return jnp.concatenate([basis_row.astype(F32), jnp.pad(state_value, ((0, 0), (0, LANE - 1)))], axis=1)


def on_device(
    basis_rows,
    reference_state,
    burning,
    coords_now,
    coords_before,
    diffusivity,
    advection,
    reaction_rate,
):
    modes = basis_rows.shape[2]
    size = lax.axis_size(SPACE)
    core = lax.axis_index(CORE).reshape(1)
    up = [(i, i + 1) for i in range(size - 1)]
    halo_low = lax.ppermute(edge_message(basis_rows[:, -1], reference_state[:, -1:]), SPACE, up)
    halo_high = lax.ppermute(
        edge_message(basis_rows[:, 0], reference_state[:, :1]), SPACE, [(j, i) for i, j in up]
    )
    jacobian, residual, own, other = rows_and_sums(
        core, diffusivity, advection, reaction_rate, basis_rows, halo_low, halo_high,
        reference_state, burning[None], coords_now, coords_before,
    )
    half = summed_over_plane(own + swapped(other))
    update = solve_update(core, half, swapped(half), modes)
    return (jacobian[None], residual[None], update)


def solution(mesh):
    split = Mesh(
        mesh.devices.reshape(8, 4, 2, mesh.shape["inst"]), ("space_0", "space_1", "space_2", "inst")
    )
    placed = (
        P(None, SPACE, None),
        P(None, SPACE),
        P(SPACE),
        P("inst", None),
        P("inst", None),
        P("inst"),
        P("inst"),
        P("inst"),
    )
    return jax.shard_map(
        on_device,
        mesh=split,
        in_specs=placed,
        out_specs=(P("inst", None, SPACE, None), P("inst", None, SPACE), P("inst", None)),
        check_vma=False,
    )
```

```python
import functools

import jax
import jax.numpy as jnp
from jax import lax
from jax.experimental import pallas as pl
from jax.experimental.pallas import tpu as pltpu
from jax.sharding import Mesh
from jax.sharding import PartitionSpec as P

PLANE = ("space_0", "space_1")
CORE = "space_2"
SPACE = (*PLANE, CORE)
F32 = jnp.float32
BF16 = jnp.bfloat16

time_step = 0.5
LANE = 128
STEP_CELLS = 512
EXACT = lax.Precision.HIGHEST


def dot_rows(a, b):
    return lax.dot_general(a, b, (((1,), (1,)), ((), ())), preferred_element_type=F32)


def dot_columns(a, b):
    return lax.dot_general(a, b, (((0,), (0,)), ((), ())), preferred_element_type=F32)


def tile_pairs(count):
    return [(i, j) for i in range(count) for j in range(i, count)]


def rows_kernel(*refs, steps, size, edges):
    refs = iter(refs)
    core_ref, nu_ref, adv_ref, rate_ref, basis_ref, before_ref, after_ref = (next(refs) for _ in range(7))
    ref_ref, burn_ref, now_ref, old_ref = (next(refs) for _ in range(4))
    if edges:
        halo_low_ref, halo_high_ref, sums_ref, right_in_ref, _, _ = (next(refs) for _ in range(6))
        jac_ref, res_ref, own_ref, other_ref, acc, right, wide = refs
    else:
        jac_ref, res_ref, acc, right, wide = refs
    step = pl.program_id(0)
    first, last = step == 0, step == pl.num_programs(0) - 1
    chunk = step * (steps - 1) if edges else step + 1
    modes = basis_ref.shape[2]
    tiles = modes // LANE
    nu, adv, rate = nu_ref[0], adv_ref[0], rate_ref[0]
    now = now_ref[...].astype(BF16)
    diff = (now_ref[...] - old_ref[...]).astype(BF16)
    now32 = now.astype(F32)
    coords = jnp.concatenate([now, diff, jnp.zeros((6, modes), BF16)], axis=0)
    start = pl.multiple_of(chunk * size, size)
    lanes = lax.broadcasted_iota(jnp.int32, (1, size), 1)
    state, moved, flux = [], [], []
    for v in range(2):
        low = before_ref[v, 15:16, :].astype(F32)
        high = after_ref[v, 0:1, :].astype(F32)
        below = pl.multiple_of(jnp.maximum(start - LANE, 0), LANE)
        above = pl.multiple_of(jnp.minimum(start + size, (steps - 1) * size), LANE)
        ref_low = ref_ref[v : v + 1, pl.ds(below, LANE)][:, LANE - 1 : LANE]
        ref_high = ref_ref[v : v + 1, pl.ds(above, LANE)][:, 0:1]
        if edges:
            low = jnp.where(first, halo_low_ref[v : v + 1, :modes], low)
            high = jnp.where(last, halo_high_ref[v : v + 1, :modes], high)
            ref_low = jnp.where(first, halo_low_ref[v : v + 1, modes : modes + 1], ref_low)
            ref_high = jnp.where(last, halo_high_ref[v : v + 1, modes : modes + 1], ref_high)
        for m in range(tiles):
            cols = slice(LANE * m, LANE * m + LANE)
            wide[v * tiles + m, 8 : 8 + size, :] = basis_ref[v, :, cols].astype(F32)
            wide[v * tiles + m, 7:8, :] = low[:, cols]
            wide[v * tiles + m, 8 + size : 9 + size, :] = high[:, cols]
        both = dot_rows(coords, basis_ref[v])
        here = ref_ref[v : v + 1, pl.ds(start, size)] + both[0:1]
        state_low = ref_low + jnp.sum(low * now32, axis=1, keepdims=True)
        state_high = ref_high + jnp.sum(high * now32, axis=1, keepdims=True)
        left = jnp.where(lanes == 0, state_low, pltpu.roll(here, 1, 1))
        following = jnp.where(lanes == size - 1, state_high, pltpu.roll(here, size - 1, 1))
        flux.append(nu * (left - 2.0 * here + following) - adv * (here - left))
        state.append(here)
        moved.append(both[1:2])
    active = burn_ref[0:1, pl.ds(start, size)].astype(F32)
    tangent = jnp.tanh(state[1])
    a = rate * active * (1.0 + tangent)
    w = a * state[0]
    e = rate * active * state[0] * (1.0 - tangent * tangent)
    res = [moved[0] - time_step * (flux[0] - w), moved[1] - time_step * (flux[1] + w)]
    res_ref[0:1, :] = res[0]
    res_ref[1:2, :] = res[1]
    mid = 1.0 + time_step * (2.0 * nu + adv)
    lower = time_step * (nu + adv)
    upper = time_step * nu

    def sides(k, lo):
        return lower * wide[k, 7 + lo : 7 + lo + LANE, :] + upper * wide[k, 9 + lo : 9 + lo + LANE, :]

    for t in range(size // LANE):
        lo = LANE * t
        a_col = jnp.broadcast_to(time_step * a[:, lo : lo + LANE], (LANE, LANE)).T
        e_col = jnp.broadcast_to(time_step * e[:, lo : lo + LANE], (LANE, LANE)).T
        fuel_own = mid + a_col
        heat_own = mid - e_col
        for m in range(tiles):
            cols = slice(LANE * m, LANE * m + LANE)
            p = wide[m, 8 + lo : 8 + lo + LANE, :]
            q = wide[tiles + m, 8 + lo : 8 + lo + LANE, :]
            fuel = fuel_own * p + e_col * q - sides(m, lo)
            heat = heat_own * q - a_col * p - sides(tiles + m, lo)
            jac_ref[0, lo : lo + LANE, cols] = fuel.astype(BF16)
            jac_ref[1, lo : lo + LANE, cols] = heat.astype(BF16)
    j0, j1 = jac_ref[0], jac_ref[1]
    r = jnp.dot(jnp.broadcast_to(res[0].astype(BF16), (8, size)), j0, preferred_element_type=F32)
    r += jnp.dot(jnp.broadcast_to(res[1].astype(BF16), (8, size)), j1, preferred_element_type=F32)
    half = modes // 2
    top = dot_columns(j0[:, :half], j0) + dot_columns(j1[:, :half], j1)
    bottom = dot_columns(j0[:, half:], j0[:, half:]) + dot_columns(j1[:, half:], j1[:, half:])

    @pl.when(first)
    def _():
        if edges:
            acc[0:half, :] = sums_ref[0:half, :] + top
            acc[half:, half:] = sums_ref[half:, half:] + bottom
            right[...] = right_in_ref[...] + r
        else:
            acc[0:half, :] = top
            acc[half:, half:] = bottom
            right[...] = r

    @pl.when(jnp.logical_not(first))
    def _():
        acc[0:half, :] += top
        acc[half:, half:] += bottom
        right[...] += r

    if not edges:
        return

    def write(target, which):
        pairs = tile_pairs(modes // LANE)
        rows_half = target.shape[0]
        base = which * rows_half
        for t, (i, j) in enumerate(pairs):
            at = LANE * t - base
            if 0 <= at < rows_half:
                target[at : at + LANE, :] = acc[LANE * i : LANE * i + LANE, LANE * j : LANE * j + LANE]
        at = LANE * len(pairs) - base
        if 0 <= at < rows_half:
            target[at:, :] = jnp.zeros((rows_half - at, LANE), F32)
            for i in range(modes // LANE):
                target[at + 8 * i : at + 8 * i + 1, :] = right[0:1, LANE * i : LANE * i + LANE]

    for core in range(2):

        @pl.when(last & (core_ref[0] == core))
        def _():
            write(own_ref, core)
            write(other_ref, 1 - core)


def packed_rows(modes):
    count = modes // LANE
    return -(-(LANE * len(tile_pairs(count)) + 8 * count) // 512) * 512


def rows_call(core, nu, adv, rate, basis, ref, burn, now, old, edge_args=None):
    cells, modes = basis.shape[1:]
    size = STEP_CELLS
    steps = cells // size
    per = size // 16
    edges = edge_args is not None
    smem = pl.BlockSpec(memory_space=pltpu.SMEM)
    half = packed_rows(modes) // 2

    def chunk(i):
        return i * (steps - 1) if edges else i + 1

    def whole(shape):
        return pl.BlockSpec(shape, lambda i: (0,) * len(shape))

    in_specs = [
        smem, smem, smem, smem,
        pl.BlockSpec((2, size, modes), lambda i: (0, chunk(i), 0)),
        pl.BlockSpec((2, 16, modes), lambda i: (0, jnp.maximum(chunk(i) * per - 1, 0), 0)),
        pl.BlockSpec((2, 16, modes), lambda i: (0, jnp.minimum(chunk(i) * per + per, cells // 16 - 1), 0)),
        whole(ref.shape), whole(burn.shape), whole(now.shape), whole(old.shape),
    ]
    out_specs = [
        pl.BlockSpec((2, size, modes), lambda i: (0, chunk(i), 0)),
        pl.BlockSpec((2, size), lambda i: (0, chunk(i))),
    ]
    out_shape = [
        jax.ShapeDtypeStruct((2, cells, modes), BF16),
        jax.ShapeDtypeStruct((2, cells), F32),
    ]
    sums_shape = [jax.ShapeDtypeStruct((modes, modes), F32), jax.ShapeDtypeStruct((8, modes), F32)]
    scratch = [pltpu.VMEM((2 * (modes // LANE), size + 16, LANE), F32)]
    args = [core, nu, adv, rate, basis, basis, basis, ref, burn, now, old]
    aliases = {}
    if edges:
        anywhere = pl.BlockSpec(memory_space=pl.ANY)
        args += edge_args
        in_specs += [whole(a.shape) for a in edge_args[:4]] + [anywhere, anywhere]
        out_specs += [whole((half, LANE))] * 2
        out_shape += [jax.ShapeDtypeStruct((half, LANE), F32)] * 2
        scratch = [pltpu.VMEM(s.shape, s.dtype) for s in sums_shape] + scratch
        aliases = {len(args) - 2: 0, len(args) - 1: 1}
    else:
        out_specs += [whole(s.shape) for s in sums_shape]
        out_shape += sums_shape
    return pl.pallas_call(
        functools.partial(rows_kernel, steps=steps, size=size, edges=edges),
        grid=(2 if edges else steps - 2,),
        in_specs=in_specs,
        out_specs=out_specs,
        out_shape=out_shape,
        scratch_shapes=scratch,
        input_output_aliases=aliases,
        compiler_params=pltpu.CompilerParams(vmem_limit_bytes=48 * 2**20),
    )(*args)


def rows_and_sums(core, nu, adv, rate, basis, halo_low, halo_high, ref, burn, now, old):
    common = (core, nu, adv, rate, basis, ref, burn, now, old)
    jacobian, residual, sums, right = rows_call(*common)
    return rows_call(*common, [halo_low, halo_high, sums, right, jacobian, residual])


def reciprocal(x):
    return pltpu.reciprocal(x, approx=True)


def inverse_block(block):
    width = block.shape[1]
    groups = [block[8 * g : 8 * g + 8] for g in range(width // 8)]
    full = (8, width)
    lanes = lax.broadcasted_iota(jnp.int32, full, 1)
    subs = lax.broadcasted_iota(jnp.int32, full, 0)
    for p in range(len(groups)):
        panel = groups[p]
        base = 8 * p
        cols = [jnp.broadcast_to(panel[:, base + j : base + j + 1], full) for j in range(8)]
        entry = [[jnp.broadcast_to(cols[t][s : s + 1], full) if t >= s else None for t in range(8)] for s in range(8)]
        window = (lanes >= base) & (lanes < base + 8)
        opened = jnp.where(window, jnp.where(lanes == subs + base, 1.0, 0.0), panel)
        rows = [jnp.broadcast_to(opened[s : s + 1], full) for s in range(8)]
        inv = []
        for j in range(8):
            inv.append(reciprocal(entry[j][j]))
            for s in [*range(j + 1, 8), *range(j)]:
                mult = (entry[j][s] if s > j else entry[s][j]) * inv[j]
                for t in range(max(s, j + 1), 8):
                    entry[s][t] = entry[s][t] - mult * entry[j][t]
                rows[s] = rows[s] - mult * rows[j]
        rows = [rows[s] * inv[s] for s in range(8)]
        for g in range(len(groups)):
            if g == p:
                continue
            terms = [jnp.broadcast_to(groups[g][:, base + s : base + s + 1], full) * rows[s] for s in range(8)]
            while len(terms) > 1:
                terms = [a + b for a, b in zip(terms[::2], terms[1::2])]
            groups[g] = jnp.where(window, 0.0, groups[g]) - terms[0]
        whole = rows[0]
        for s in range(1, 8):
            whole = jnp.where(subs == s, rows[s], whole)
        groups[p] = whole
    return jnp.concatenate(groups, axis=0)


def exact_dot(a, b, dims=((1,), (0,))):
    return lax.dot_general(a, b, (dims, ((), ())), precision=EXACT, preferred_element_type=F32)


def solve_kernel(core_ref, own_ref, other_ref, out_ref, packed, work, panel, *, count):
    half = own_ref.shape[0]
    core = core_ref[0]
    packed[pl.ds(pl.multiple_of(core * half, half), half), :] = own_ref[...]
    packed[pl.ds(pl.multiple_of((1 - core) * half, half), half), :] = other_ref[...]
    modes = count * LANE
    pairs = tile_pairs(count)
    for t, (i, j) in enumerate(pairs):
        work[LANE * i : LANE * i + LANE, LANE * j : LANE * j + LANE] = packed[LANE * t : LANE * t + LANE, :]
    for i in range(count):
        at = LANE * len(pairs) + 8 * i
        r = jnp.broadcast_to(packed[at : at + 1, :] + packed[at + 1 : at + 2, :], (LANE, LANE))
        work[LANE * i : LANE * i + LANE, modes : modes + LANE] = r.T
    for k in range(count):
        lo = LANE * k
        end = lo + LANE
        x = exact_dot(inverse_block(work[lo:end, lo:end]), work[lo:end, end:])
        panel[lo:end, end:] = x
        for i in range(k + 1, count):
            a = LANE * i
            work[a : a + LANE, a:] -= exact_dot(work[lo:end, a : a + LANE], x[:, a - end :], ((0,), (0,)))
    solved = {}
    for k in reversed(range(count)):
        lo = LANE * k
        u = panel[lo : lo + LANE, modes:]
        for i in range(k + 1, count):
            u = u - exact_dot(panel[lo : lo + LANE, LANE * i : LANE * i + LANE], solved[i])
        solved[k] = u
        out_ref[0:1, lo : lo + LANE] = -u.T[0:1]


def solve_update(core, own, other, modes):
    vmem = pl.BlockSpec(memory_space=pltpu.VMEM)
    return pl.pallas_call(
        functools.partial(solve_kernel, count=modes // LANE),
        out_shape=jax.ShapeDtypeStruct((1, modes), F32),
        in_specs=[pl.BlockSpec(memory_space=pltpu.SMEM), vmem, vmem],
        out_specs=vmem,
        scratch_shapes=[
            pltpu.VMEM((2 * own.shape[0], LANE), F32),
            pltpu.VMEM((modes, modes + LANE), F32),
            pltpu.VMEM((modes, modes + LANE), F32),
        ],
        compiler_params=pltpu.CompilerParams(vmem_limit_bytes=48 * 2**20),
    )(core, own, other)


def swapped(shard):
    return lax.ppermute(shard, CORE, [(0, 1), (1, 0)])


def summed_over_plane(shard, low_rows):
    count = lax.axis_size(PLANE)
    rounded = shard.astype(BF16)
    left_over = jnp.roll(shard - rounded.astype(F32), 1, axis=0).astype(BF16)
    sent = jnp.where(low_rows, left_over, rounded)
    blocks = sent.reshape(count, shard.shape[0] // count, shard.shape[1])
    mine = jnp.sum(lax.all_to_all(blocks, PLANE, 0, 0, tiled=True).astype(F32), axis=0)
    copies = jnp.broadcast_to(mine, blocks.shape)
    return lax.all_to_all(copies, PLANE, 0, 0, tiled=True).reshape(shard.shape)


def edge_message(basis_row, state_value):
    return jnp.concatenate([basis_row.astype(F32), jnp.pad(state_value, ((0, 0), (0, LANE - 1)))], axis=1)


def on_device(
    basis_rows,
    reference_state,
    burning,
    coords_now,
    coords_before,
    diffusivity,
    advection,
    reaction_rate,
):
    modes = basis_rows.shape[2]
    size = lax.axis_size(SPACE)
    core = lax.axis_index(CORE).reshape(1)
    up = [(i, i + 1) for i in range(size - 1)]
    halo_low = lax.ppermute(edge_message(basis_rows[:, -1], reference_state[:, -1:]), SPACE, up)
    halo_high = lax.ppermute(
        edge_message(basis_rows[:, 0], reference_state[:, :1]), SPACE, [(j, i) for i, j in up]
    )
    jacobian, residual, own, other = rows_and_sums(
        core, diffusivity, advection, reaction_rate, basis_rows, halo_low, halo_high,
        reference_state, burning[None], coords_now, coords_before,
    )
    row = core * own.shape[0] + jnp.arange(own.shape[0], dtype=jnp.int32)
    begin = LANE * len(tile_pairs(modes // LANE))
    low_rows = ((row >= begin) & (row % 8 == 1))[:, None]
    half = summed_over_plane(own + swapped(other), low_rows)
    update = solve_update(core, half, swapped(half), modes)
    return (jacobian[None], residual[None], update)


def solution(mesh):
    split = Mesh(
        mesh.devices.reshape(8, 4, 2, mesh.shape["inst"]), ("space_0", "space_1", "space_2", "inst")
    )
    placed = (
        P(None, SPACE, None),
        P(None, SPACE),
        P(SPACE),
        P("inst", None),
        P("inst", None),
        P("inst"),
        P("inst"),
        P("inst"),
    )
    return jax.shard_map(
        on_device,
        mesh=split,
        in_specs=placed,
        out_specs=(P("inst", None, SPACE, None), P("inst", None, SPACE), P("inst", None)),
        check_vma=False,
    )
```

```python
import functools

import jax
import jax.numpy as jnp
from jax import lax
from jax.experimental import pallas as pl
from jax.experimental.pallas import tpu as pltpu
from jax.sharding import Mesh
from jax.sharding import PartitionSpec as P

PLANE = ("space_0", "space_1")
CORE = "space_2"
SPACE = (*PLANE, CORE)
F32 = jnp.float32
BF16 = jnp.bfloat16

time_step = 0.5
LANE = 128
STEP_CELLS = 768
GRAM_TILES = 2
EXACT = lax.Precision.HIGHEST


def dot_rows(a, b):
    return lax.dot_general(a, b, (((1,), (1,)), ((), ())), preferred_element_type=F32)


def dot_columns(a, b):
    return lax.dot_general(a, b, (((0,), (0,)), ((), ())), preferred_element_type=F32)


def tile_pairs(count):
    return [(i, j) for i in range(count) for j in range(i, count)]


def rows_kernel(*refs, steps, size, edges):
    refs = iter(refs)
    rates_ref, basis_ref, before_ref, after_ref = (next(refs) for _ in range(4))
    ref_ref, burn_ref, now_ref, old_ref = (next(refs) for _ in range(4))
    if edges:
        core_ref, halo_low_ref, halo_high_ref, sums_ref, right_in_ref, _, _ = (next(refs) for _ in range(7))
        jac_ref, res_ref, own_ref, other_ref, acc, right, wide = refs
    else:
        jac_ref, res_ref, acc, right, wide = refs
    step = pl.program_id(0)
    first, last = step == 0, step == pl.num_programs(0) - 1
    chunk = step * (steps - 1) if edges else step + 1
    modes = basis_ref.shape[2]
    tiles = modes // LANE
    nu, adv, rate = (rates_ref[i : i + 1, 0:1] for i in range(3))
    nu_row, adv_row = rates_ref[0:1, :], rates_ref[1:2, :]
    now = now_ref[...].astype(BF16)
    diff = (now_ref[...] - old_ref[...]).astype(BF16)
    now32 = now.astype(F32)
    coords = jnp.concatenate([now, diff, jnp.zeros((6, modes), BF16)], axis=0)
    start = pl.multiple_of(chunk * size, size)
    lanes = lax.broadcasted_iota(jnp.int32, (1, size), 1)
    state, moved, flux = [], [], []
    for v in range(2):
        low = before_ref[v, 15:16, :].astype(F32)
        high = after_ref[v, 0:1, :].astype(F32)
        below = pl.multiple_of(jnp.maximum(start - LANE, 0), LANE)
        above = pl.multiple_of(jnp.minimum(start + size, (steps - 1) * size), LANE)
        ref_low = ref_ref[v : v + 1, pl.ds(below, LANE)][:, LANE - 1 : LANE]
        ref_high = ref_ref[v : v + 1, pl.ds(above, LANE)][:, 0:1]
        if edges:
            low = jnp.where(first, halo_low_ref[v : v + 1, :modes], low)
            high = jnp.where(last, halo_high_ref[v : v + 1, :modes], high)
            ref_low = jnp.where(first, halo_low_ref[v : v + 1, modes : modes + 1], ref_low)
            ref_high = jnp.where(last, halo_high_ref[v : v + 1, modes : modes + 1], ref_high)
        for m in range(tiles):
            cols = slice(LANE * m, LANE * m + LANE)
            wide[v * tiles + m, 8 : 8 + size, :] = basis_ref[v, :, cols].astype(F32)
            wide[v * tiles + m, 7:8, :] = low[:, cols]
            wide[v * tiles + m, 8 + size : 9 + size, :] = high[:, cols]
        both = dot_rows(coords, basis_ref[v])
        here = ref_ref[v : v + 1, pl.ds(start, size)] + both[0:1]
        state_low = ref_low + jnp.sum(low * now32, axis=1, keepdims=True)
        state_high = ref_high + jnp.sum(high * now32, axis=1, keepdims=True)
        left = jnp.where(lanes == 0, state_low, pltpu.roll(here, 1, 1))
        following = jnp.where(lanes == size - 1, state_high, pltpu.roll(here, size - 1, 1))
        flux.append(nu * (left - 2.0 * here + following) - adv * (here - left))
        state.append(here)
        moved.append(both[1:2])
    active = burn_ref[0:1, pl.ds(start, size)].astype(F32)
    tangent = jnp.tanh(state[1])
    a = rate * active * (1.0 + tangent)
    w = a * state[0]
    e = rate * active * state[0] * (1.0 - tangent * tangent)
    res = [moved[0] - time_step * (flux[0] - w), moved[1] - time_step * (flux[1] + w)]
    res_ref[0:1, :] = res[0]
    res_ref[1:2, :] = res[1]
    mid = 1.0 + time_step * (2.0 * nu_row + adv_row)
    lower = time_step * (nu_row + adv_row)
    upper = time_step * nu_row

    def sides(k, lo):
        return lower * wide[k, 7 + lo : 7 + lo + LANE, :] + upper * wide[k, 9 + lo : 9 + lo + LANE, :]

    half = modes // 2

    @pl.when(first)
    def _():
        if edges:
            acc[0:half, :] = sums_ref[0:half, :]
            acc[half:, half:] = sums_ref[half:, half:]
            right[...] = right_in_ref[...]
        else:
            acc[...] = jnp.zeros_like(acc)
            right[...] = jnp.zeros_like(right)

    rounded = [jnp.broadcast_to(x.astype(BF16), (8, size)) for x in res]
    for t in range(size // LANE):
        lo = LANE * t
        a_col = jnp.broadcast_to(time_step * a[:, lo : lo + LANE], (LANE, LANE)).T
        e_col = jnp.broadcast_to(time_step * e[:, lo : lo + LANE], (LANE, LANE)).T
        fuel_own = mid + a_col
        heat_own = mid - e_col
        for m in range(tiles):
            cols = slice(LANE * m, LANE * m + LANE)
            p = wide[m, 8 + lo : 8 + lo + LANE, :]
            q = wide[tiles + m, 8 + lo : 8 + lo + LANE, :]
            fuel = fuel_own * p + e_col * q - sides(m, lo)
            heat = heat_own * q - a_col * p - sides(tiles + m, lo)
            jac_ref[0, lo : lo + LANE, cols] = fuel.astype(BF16)
            jac_ref[1, lo : lo + LANE, cols] = heat.astype(BF16)
        if (t + 1) % GRAM_TILES == 0:
            span = slice(lo + LANE - GRAM_TILES * LANE, lo + LANE)
            j = jnp.concatenate([jac_ref[0, span, :], jac_ref[1, span, :]], axis=0)
            both_res = jnp.concatenate([x[:, span] for x in rounded], axis=1)
            right[...] += jnp.dot(both_res, j, preferred_element_type=F32)
            acc[0:half, :] += dot_columns(j[:, :half], j)
            acc[half:, half:] += dot_columns(j[:, half:], j[:, half:])

    if not edges:
        return

    def write(target, which):
        pairs = tile_pairs(modes // LANE)
        rows_half = target.shape[0]
        base = which * rows_half
        for t, (i, j) in enumerate(pairs):
            at = LANE * t - base
            if 0 <= at < rows_half:
                target[at : at + LANE, :] = acc[LANE * i : LANE * i + LANE, LANE * j : LANE * j + LANE]
        at = LANE * len(pairs) - base
        if 0 <= at < rows_half:
            target[at:, :] = jnp.zeros((rows_half - at, LANE), F32)
            for i in range(modes // LANE):
                target[at + 8 * i : at + 8 * i + 1, :] = right[0:1, LANE * i : LANE * i + LANE]

    for core in range(2):

        @pl.when(last & (core_ref[0] == core))
        def _():
            write(own_ref, core)
            write(other_ref, 1 - core)


def packed_rows(modes):
    count = modes // LANE
    return -(-(LANE * len(tile_pairs(count)) + 8 * count) // 512) * 512


def rows_call(rates, basis, ref, burn, now, old, edge_args=None):
    cells, modes = basis.shape[1:]
    size = STEP_CELLS
    steps = cells // size
    per = size // 16
    edges = edge_args is not None
    smem = pl.BlockSpec(memory_space=pltpu.SMEM)
    half = packed_rows(modes) // 2

    def chunk(i):
        return i * (steps - 1) if edges else i + 1

    def whole(shape):
        return pl.BlockSpec(shape, lambda i: (0,) * len(shape))

    in_specs = [
        whole(rates.shape),
        pl.BlockSpec((2, size, modes), lambda i: (0, chunk(i), 0)),
        pl.BlockSpec((2, 16, modes), lambda i: (0, jnp.maximum(chunk(i) * per - 1, 0), 0)),
        pl.BlockSpec((2, 16, modes), lambda i: (0, jnp.minimum(chunk(i) * per + per, cells // 16 - 1), 0)),
        whole(ref.shape), whole(burn.shape), whole(now.shape), whole(old.shape),
    ]
    out_specs = [
        pl.BlockSpec((2, size, modes), lambda i: (0, chunk(i), 0)),
        pl.BlockSpec((2, size), lambda i: (0, chunk(i))),
    ]
    out_shape = [
        jax.ShapeDtypeStruct((2, cells, modes), BF16),
        jax.ShapeDtypeStruct((2, cells), F32),
    ]
    sums_shape = [jax.ShapeDtypeStruct((modes, modes), F32), jax.ShapeDtypeStruct((8, modes), F32)]
    scratch = [pltpu.VMEM((2 * (modes // LANE), size + 16, LANE), F32)]
    args = [rates, basis, basis, basis, ref, burn, now, old]
    aliases = {}
    if edges:
        anywhere = pl.BlockSpec(memory_space=pl.ANY)
        args += edge_args
        in_specs += [smem] + [whole(a.shape) for a in edge_args[1:5]] + [anywhere, anywhere]
        out_specs += [whole((half, LANE))] * 2
        out_shape += [jax.ShapeDtypeStruct((half, LANE), F32)] * 2
        scratch = [pltpu.VMEM(s.shape, s.dtype) for s in sums_shape] + scratch
        aliases = {len(args) - 2: 0, len(args) - 1: 1}
    else:
        out_specs += [whole(s.shape) for s in sums_shape]
        out_shape += sums_shape
    return pl.pallas_call(
        functools.partial(rows_kernel, steps=steps, size=size, edges=edges),
        grid=(2 if edges else steps - 2,),
        in_specs=in_specs,
        out_specs=out_specs,
        out_shape=out_shape,
        scratch_shapes=scratch,
        input_output_aliases=aliases,
        compiler_params=pltpu.CompilerParams(vmem_limit_bytes=60 * 2**20),
    )(*args)


def rows_and_sums(core, rates, basis, halo_low, halo_high, ref, burn, now, old):
    common = (rates, basis, ref, burn, now, old)
    jacobian, residual, sums, right = rows_call(*common)
    return rows_call(*common, [core, halo_low, halo_high, sums, right, jacobian, residual])


def reciprocal(x):
    return pltpu.reciprocal(x, approx=True)


def inverse_block(block):
    width = block.shape[1]
    groups = [block[8 * g : 8 * g + 8] for g in range(width // 8)]
    full = (8, width)
    lanes = lax.broadcasted_iota(jnp.int32, full, 1)
    subs = lax.broadcasted_iota(jnp.int32, full, 0)
    for p in range(len(groups)):
        panel = groups[p]
        base = 8 * p
        cols = [jnp.broadcast_to(panel[:, base + j : base + j + 1], full) for j in range(8)]
        entry = [[jnp.broadcast_to(cols[t][s : s + 1], full) if t >= s else None for t in range(8)] for s in range(8)]
        window = (lanes >= base) & (lanes < base + 8)
        opened = jnp.where(window, jnp.where(lanes == subs + base, 1.0, 0.0), panel)
        rows = [jnp.broadcast_to(opened[s : s + 1], full) for s in range(8)]
        inv = []
        for j in range(8):
            inv.append(reciprocal(entry[j][j]))
            for s in [*range(j + 1, 8), *range(j)]:
                mult = (entry[j][s] if s > j else entry[s][j]) * inv[j]
                for t in range(max(s, j + 1), 8):
                    entry[s][t] = entry[s][t] - mult * entry[j][t]
                rows[s] = rows[s] - mult * rows[j]
        rows = [rows[s] * inv[s] for s in range(8)]
        for g in range(len(groups)):
            if g == p:
                continue
            terms = [jnp.broadcast_to(groups[g][:, base + s : base + s + 1], full) * rows[s] for s in range(8)]
            while len(terms) > 1:
                terms = [a + b for a, b in zip(terms[::2], terms[1::2])]
            groups[g] = jnp.where(window, 0.0, groups[g]) - terms[0]
        whole = rows[0]
        for s in range(1, 8):
            whole = jnp.where(subs == s, rows[s], whole)
        groups[p] = whole
    return jnp.concatenate(groups, axis=0)


def exact_dot(a, b, dims=((1,), (0,))):
    return lax.dot_general(a, b, (dims, ((), ())), precision=EXACT, preferred_element_type=F32)


def solve_kernel(core_ref, own_ref, other_ref, out_ref, packed, work, panel, *, count):
    half = own_ref.shape[0]
    core = core_ref[0]
    packed[pl.ds(pl.multiple_of(core * half, half), half), :] = own_ref[...]
    packed[pl.ds(pl.multiple_of((1 - core) * half, half), half), :] = other_ref[...]
    modes = count * LANE
    pairs = tile_pairs(count)
    for t, (i, j) in enumerate(pairs):
        work[LANE * i : LANE * i + LANE, LANE * j : LANE * j + LANE] = packed[LANE * t : LANE * t + LANE, :]
    for i in range(count):
        at = LANE * len(pairs) + 8 * i
        r = jnp.broadcast_to(packed[at : at + 1, :] + packed[at + 1 : at + 2, :], (LANE, LANE))
        work[LANE * i : LANE * i + LANE, modes : modes + LANE] = r.T
    for k in range(count):
        lo = LANE * k
        end = lo + LANE
        x = exact_dot(inverse_block(work[lo:end, lo:end]), work[lo:end, end:])
        panel[lo:end, end:] = x
        for i in range(k + 1, count):
            a = LANE * i
            work[a : a + LANE, a:] -= exact_dot(work[lo:end, a : a + LANE], x[:, a - end :], ((0,), (0,)))
    solved = {}
    for k in reversed(range(count)):
        lo = LANE * k
        u = panel[lo : lo + LANE, modes:]
        for i in range(k + 1, count):
            u = u - exact_dot(panel[lo : lo + LANE, LANE * i : LANE * i + LANE], solved[i])
        solved[k] = u
        out_ref[0:1, lo : lo + LANE] = -u.T[0:1]


def solve_update(core, own, other, modes):
    vmem = pl.BlockSpec(memory_space=pltpu.VMEM)
    return pl.pallas_call(
        functools.partial(solve_kernel, count=modes // LANE),
        out_shape=jax.ShapeDtypeStruct((1, modes), F32),
        in_specs=[pl.BlockSpec(memory_space=pltpu.SMEM), vmem, vmem],
        out_specs=vmem,
        scratch_shapes=[
            pltpu.VMEM((2 * own.shape[0], LANE), F32),
            pltpu.VMEM((modes, modes + LANE), F32),
            pltpu.VMEM((modes, modes + LANE), F32),
        ],
        compiler_params=pltpu.CompilerParams(vmem_limit_bytes=48 * 2**20),
    )(core, own, other)


def swapped(shard):
    return lax.ppermute(shard, CORE, [(0, 1), (1, 0)])


def summed_over_plane(shard, low_rows):
    count = lax.axis_size(PLANE)
    rounded = shard.astype(BF16)
    left_over = jnp.roll(shard - rounded.astype(F32), 1, axis=0).astype(BF16)
    sent = jnp.where(low_rows, left_over, rounded)
    blocks = sent.reshape(count, shard.shape[0] // count, shard.shape[1])
    mine = jnp.sum(lax.all_to_all(blocks, PLANE, 0, 0, tiled=True).astype(F32), axis=0)
    copies = jnp.broadcast_to(mine, blocks.shape)
    return lax.all_to_all(copies, PLANE, 0, 0, tiled=True).reshape(shard.shape)


def edge_kernel(
    nu_ref, adv_ref, rate_ref, first_ref, last_ref, ref_first, ref_last, up_ref, down_ref, rates_ref
):
    modes = first_ref.shape[2]
    for v in range(2):
        up_ref[v : v + 1, :modes] = last_ref[v].astype(F32)[15:16]
        down_ref[v : v + 1, :modes] = first_ref[v].astype(F32)[0:1]
    up_ref[:, modes:] = jnp.broadcast_to(ref_last[:, LANE - 1 : LANE], (2, LANE))
    down_ref[:, modes:] = jnp.broadcast_to(ref_first[:, 0:1], (2, LANE))
    for i, scalar_ref in enumerate((nu_ref, adv_ref, rate_ref)):
        rates_ref[i : i + 1, :] = jnp.full((1, LANE), scalar_ref[0], F32)


def edge_messages(basis, ref, nu, adv, rate):
    cells, modes = basis.shape[1:]
    smem = pl.BlockSpec(memory_space=pltpu.SMEM)

    def whole(shape):
        return pl.BlockSpec(shape, lambda i: (0,) * len(shape))

    shapes = [(2, modes + LANE), (2, modes + LANE), (8, LANE)]
    return pl.pallas_call(
        edge_kernel,
        grid=(1,),
        in_specs=[
            smem, smem, smem,
            pl.BlockSpec((2, 16, modes), lambda i: (0, 0, 0)),
            pl.BlockSpec((2, 16, modes), lambda i: (0, cells // 16 - 1, 0)),
            pl.BlockSpec((2, LANE), lambda i: (0, 0)),
            pl.BlockSpec((2, LANE), lambda i: (0, cells // LANE - 1)),
        ],
        out_specs=[whole(shape) for shape in shapes],
        out_shape=[jax.ShapeDtypeStruct(shape, F32) for shape in shapes],
        compiler_params=pltpu.CompilerParams(vmem_limit_bytes=60 * 2**20),
    )(nu, adv, rate, basis, basis, ref, ref)


def on_device(
    basis_rows,
    reference_state,
    burning,
    coords_now,
    coords_before,
    diffusivity,
    advection,
    reaction_rate,
):
    modes = basis_rows.shape[2]
    size = lax.axis_size(SPACE)
    core = lax.axis_index(CORE).reshape(1)
    up = [(i, i + 1) for i in range(size - 1)]
    up_row, down_row, rates = edge_messages(basis_rows, reference_state, diffusivity, advection, reaction_rate)
    halo_low = lax.ppermute(up_row, SPACE, up)
    halo_high = lax.ppermute(down_row, SPACE, [(j, i) for i, j in up])
    jacobian, residual, own, other = rows_and_sums(
        core, rates, basis_rows, halo_low, halo_high, reference_state, burning[None], coords_now, coords_before
    )
    row = core * own.shape[0] + jnp.arange(own.shape[0], dtype=jnp.int32)
    begin = LANE * len(tile_pairs(modes // LANE))
    low_rows = ((row >= begin) & (row % 8 == 1))[:, None]
    half = summed_over_plane(own + swapped(other), low_rows)
    update = solve_update(core, half, swapped(half), modes)
    return (jacobian[None], residual[None], update)


def solution(mesh):
    split = Mesh(
        mesh.devices.reshape(8, 4, 2, mesh.shape["inst"]), ("space_0", "space_1", "space_2", "inst")
    )
    placed = (
        P(None, SPACE, None),
        P(None, SPACE),
        P(SPACE),
        P("inst", None),
        P("inst", None),
        P("inst"),
        P("inst"),
        P("inst"),
    )
    return jax.shard_map(
        on_device,
        mesh=split,
        in_specs=placed,
        out_specs=(P("inst", None, SPACE, None), P("inst", None, SPACE), P("inst", None)),
        check_vma=False,
    )
```

```python
import functools

import jax
import jax.numpy as jnp
from jax import lax
from jax.experimental import pallas as pl
from jax.experimental.pallas import tpu as pltpu
from jax.sharding import Mesh
from jax.sharding import PartitionSpec as P

PLANE = ("space_0", "space_1")
CORE = "space_2"
SPACE = (*PLANE, CORE)
F32 = jnp.float32
BF16 = jnp.bfloat16

time_step = 0.5
LANE = 128
STEP_CELLS = 768
GRAM_TILES = 2
EXACT = lax.Precision.HIGHEST


def dot_rows(a, b):
    return lax.dot_general(a, b, (((1,), (1,)), ((), ())), preferred_element_type=F32)


def dot_columns(a, b):
    return lax.dot_general(a, b, (((0,), (0,)), ((), ())), preferred_element_type=F32)


def tile_pairs(count):
    return [(i, j) for i in range(count) for j in range(i, count)]


def rows_kernel(*refs, steps, size, edges):
    refs = iter(refs)
    rates_ref, basis_ref, before_ref, after_ref = (next(refs) for _ in range(4))
    ref_ref, burn_ref, now_ref, old_ref = (next(refs) for _ in range(4))
    if edges:
        core_ref, halo_low_ref, halo_high_ref, sums_ref, right_in_ref, _, _ = (next(refs) for _ in range(7))
        jac_ref, res_ref, own_ref, other_ref, acc, right, wide = refs
    else:
        jac_ref, res_ref, acc, right, wide = refs
    step = pl.program_id(0)
    first, last = step == 0, step == pl.num_programs(0) - 1
    chunk = step * (steps - 1) if edges else step + 1
    modes = basis_ref.shape[2]
    tiles = modes // LANE
    nu, adv, rate = (rates_ref[i : i + 1, 0:1] for i in range(3))
    nu_row, adv_row = rates_ref[0:1, :], rates_ref[1:2, :]
    now = now_ref[...].astype(BF16)
    diff = (now_ref[...] - old_ref[...]).astype(BF16)
    now32 = now.astype(F32)
    coords = jnp.concatenate([now, diff, jnp.zeros((6, modes), BF16)], axis=0)
    start = pl.multiple_of(chunk * size, size)
    lanes = lax.broadcasted_iota(jnp.int32, (1, size), 1)
    state, moved, flux = [], [], []
    for v in range(2):
        low = before_ref[v, 15:16, :].astype(F32)
        high = after_ref[v, 0:1, :].astype(F32)
        below = pl.multiple_of(jnp.maximum(start - LANE, 0), LANE)
        above = pl.multiple_of(jnp.minimum(start + size, (steps - 1) * size), LANE)
        ref_low = ref_ref[v : v + 1, pl.ds(below, LANE)][:, LANE - 1 : LANE]
        ref_high = ref_ref[v : v + 1, pl.ds(above, LANE)][:, 0:1]
        if edges:
            low = jnp.where(first, halo_low_ref[v : v + 1, :modes], low)
            high = jnp.where(last, halo_high_ref[v : v + 1, :modes], high)
            ref_low = jnp.where(first, halo_low_ref[v : v + 1, modes : modes + 1], ref_low)
            ref_high = jnp.where(last, halo_high_ref[v : v + 1, modes : modes + 1], ref_high)
        for m in range(tiles):
            cols = slice(LANE * m, LANE * m + LANE)
            wide[v * tiles + m, 8 : 8 + size, :] = basis_ref[v, :, cols].astype(F32)
            wide[v * tiles + m, 7:8, :] = low[:, cols]
            wide[v * tiles + m, 8 + size : 9 + size, :] = high[:, cols]
        both = dot_rows(coords, basis_ref[v])
        here = ref_ref[v : v + 1, pl.ds(start, size)] + both[0:1]
        state_low = ref_low + jnp.sum(low * now32, axis=1, keepdims=True)
        state_high = ref_high + jnp.sum(high * now32, axis=1, keepdims=True)
        left = jnp.where(lanes == 0, state_low, pltpu.roll(here, 1, 1))
        following = jnp.where(lanes == size - 1, state_high, pltpu.roll(here, size - 1, 1))
        flux.append(nu * (left - 2.0 * here + following) - adv * (here - left))
        state.append(here)
        moved.append(both[1:2])
    active = burn_ref[0:1, pl.ds(start, size)].astype(F32)
    tangent = jnp.tanh(state[1])
    a = rate * active * (1.0 + tangent)
    w = a * state[0]
    e = rate * active * state[0] * (1.0 - tangent * tangent)
    res = [moved[0] - time_step * (flux[0] - w), moved[1] - time_step * (flux[1] + w)]
    res_ref[0:1, :] = res[0]
    res_ref[1:2, :] = res[1]
    mid = 1.0 + time_step * (2.0 * nu_row + adv_row)
    lower = time_step * (nu_row + adv_row)
    upper = time_step * nu_row

    def sides(k, lo):
        return lower * wide[k, 7 + lo : 7 + lo + LANE, :] + upper * wide[k, 9 + lo : 9 + lo + LANE, :]

    half = modes // 2

    @pl.when(first)
    def _():
        if edges:
            acc[0:half, :] = sums_ref[0:half, :]
            acc[half:, half:] = sums_ref[half:, half:]
            right[...] = right_in_ref[...]
        else:
            acc[...] = jnp.zeros_like(acc)
            right[...] = jnp.zeros_like(right)

    rounded = [jnp.broadcast_to(x.astype(BF16), (8, size)) for x in res]
    for t in range(size // LANE):
        lo = LANE * t
        a_col = jnp.broadcast_to(time_step * a[:, lo : lo + LANE], (LANE, LANE)).T
        e_col = jnp.broadcast_to(time_step * e[:, lo : lo + LANE], (LANE, LANE)).T
        fuel_own = mid + a_col
        heat_own = mid - e_col
        for m in range(tiles):
            cols = slice(LANE * m, LANE * m + LANE)
            p = wide[m, 8 + lo : 8 + lo + LANE, :]
            q = wide[tiles + m, 8 + lo : 8 + lo + LANE, :]
            fuel = fuel_own * p + e_col * q - sides(m, lo)
            heat = heat_own * q - a_col * p - sides(tiles + m, lo)
            jac_ref[0, lo : lo + LANE, cols] = fuel.astype(BF16)
            jac_ref[1, lo : lo + LANE, cols] = heat.astype(BF16)
        if (t + 1) % GRAM_TILES == 0:
            span = slice(lo + LANE - GRAM_TILES * LANE, lo + LANE)
            j = jnp.concatenate([jac_ref[0, span, :], jac_ref[1, span, :]], axis=0)
            both_res = jnp.concatenate([x[:, span] for x in rounded], axis=1)
            right[...] += jnp.dot(both_res, j, preferred_element_type=F32)
            acc[0:half, :] += dot_columns(j[:, :half], j)
            acc[half:, half:] += dot_columns(j[:, half:], j[:, half:])

    if not edges:
        return

    def write(target, which):
        pairs = tile_pairs(modes // LANE)
        rows_half = target.shape[0]
        base = which * rows_half
        for t, (i, j) in enumerate(pairs):
            at = LANE * t - base
            if 0 <= at < rows_half:
                target[at : at + LANE, :] = acc[LANE * i : LANE * i + LANE, LANE * j : LANE * j + LANE]
        at = LANE * len(pairs) - base
        if 0 <= at < rows_half:
            target[at:, :] = jnp.zeros((rows_half - at, LANE), F32)
            for i in range(modes // LANE):
                target[at + 8 * i : at + 8 * i + 1, :] = right[0:1, LANE * i : LANE * i + LANE]

    for core in range(2):

        @pl.when(last & (core_ref[0] == core))
        def _():
            write(own_ref, core)
            write(other_ref, 1 - core)


def packed_rows(modes):
    count = modes // LANE
    return -(-(LANE * len(tile_pairs(count)) + 8 * count) // 512) * 512


def rows_call(rates, basis, ref, burn, now, old, edge_args=None):
    cells, modes = basis.shape[1:]
    size = STEP_CELLS
    steps = cells // size
    per = size // 16
    edges = edge_args is not None
    smem = pl.BlockSpec(memory_space=pltpu.SMEM)
    half = packed_rows(modes) // 2

    def chunk(i):
        return i * (steps - 1) if edges else i + 1

    def whole(shape):
        return pl.BlockSpec(shape, lambda i: (0,) * len(shape))

    in_specs = [
        whole(rates.shape),
        pl.BlockSpec((2, size, modes), lambda i: (0, chunk(i), 0)),
        pl.BlockSpec((2, 16, modes), lambda i: (0, jnp.maximum(chunk(i) * per - 1, 0), 0)),
        pl.BlockSpec((2, 16, modes), lambda i: (0, jnp.minimum(chunk(i) * per + per, cells // 16 - 1), 0)),
        whole(ref.shape), whole(burn.shape), whole(now.shape), whole(old.shape),
    ]
    out_specs = [
        pl.BlockSpec((2, size, modes), lambda i: (0, chunk(i), 0)),
        pl.BlockSpec((2, size), lambda i: (0, chunk(i))),
    ]
    out_shape = [
        jax.ShapeDtypeStruct((2, cells, modes), BF16),
        jax.ShapeDtypeStruct((2, cells), F32),
    ]
    sums_shape = [jax.ShapeDtypeStruct((modes, modes), F32), jax.ShapeDtypeStruct((8, modes), F32)]
    scratch = [pltpu.VMEM((2 * (modes // LANE), size + 16, LANE), F32)]
    args = [rates, basis, basis, basis, ref, burn, now, old]
    aliases = {}
    if edges:
        anywhere = pl.BlockSpec(memory_space=pl.ANY)
        args += edge_args
        in_specs += [smem] + [whole(a.shape) for a in edge_args[1:5]] + [anywhere, anywhere]
        out_specs += [whole((half, LANE))] * 2
        out_shape += [jax.ShapeDtypeStruct((half, LANE), F32)] * 2
        scratch = [pltpu.VMEM(s.shape, s.dtype) for s in sums_shape] + scratch
        aliases = {len(args) - 2: 0, len(args) - 1: 1}
    else:
        out_specs += [whole(s.shape) for s in sums_shape]
        out_shape += sums_shape
    return pl.pallas_call(
        functools.partial(rows_kernel, steps=steps, size=size, edges=edges),
        grid=(2 if edges else steps - 2,),
        in_specs=in_specs,
        out_specs=out_specs,
        out_shape=out_shape,
        scratch_shapes=scratch,
        input_output_aliases=aliases,
        compiler_params=pltpu.CompilerParams(vmem_limit_bytes=(48 if edges else 60) * 2**20),
    )(*args)


def rows_and_sums(core, rates, basis, halo_low, halo_high, ref, burn, now, old):
    common = (rates, basis, ref, burn, now, old)
    jacobian, residual, sums, right = rows_call(*common)
    return rows_call(*common, [core, halo_low, halo_high, sums, right, jacobian, residual])


def reciprocal(x):
    return pltpu.reciprocal(x, approx=True)


def inverse_block(block):
    width = block.shape[1]
    groups = [block[8 * g : 8 * g + 8] for g in range(width // 8)]
    full = (8, width)
    lanes = lax.broadcasted_iota(jnp.int32, full, 1)
    subs = lax.broadcasted_iota(jnp.int32, full, 0)
    for p in range(len(groups)):
        panel = groups[p]
        base = 8 * p
        cols = [jnp.broadcast_to(panel[:, base + j : base + j + 1], full) for j in range(8)]
        window = (lanes >= base) & (lanes < base + 8)
        opened = jnp.where(window, jnp.where(lanes == subs + base, 1.0, 0.0), panel)
        scale = jnp.zeros(full, F32)
        for j in range(8):
            inv = reciprocal(jnp.broadcast_to(cols[j][j : j + 1], full))
            mult = jnp.where(subs == j, 0.0, cols[j]) * inv
            scale = jnp.where(subs == j, inv, scale)
            for t in range(j + 1, 8):
                cols[t] = cols[t] - mult * jnp.broadcast_to(cols[t][j : j + 1], full)
            opened = opened - mult * jnp.broadcast_to(opened[j : j + 1], full)
        whole = opened * scale
        rows = [jnp.broadcast_to(whole[s : s + 1], full) for s in range(8)]
        for g in range(len(groups)):
            if g == p:
                continue
            terms = [jnp.broadcast_to(groups[g][:, base + s : base + s + 1], full) * rows[s] for s in range(8)]
            while len(terms) > 1:
                terms = [a + b for a, b in zip(terms[::2], terms[1::2])]
            groups[g] = jnp.where(window, 0.0, groups[g]) - terms[0]
        groups[p] = whole
    return jnp.concatenate(groups, axis=0)


def exact_dot(a, b, dims=((1,), (0,))):
    return lax.dot_general(a, b, (dims, ((), ())), precision=EXACT, preferred_element_type=F32)


def solve_kernel(core_ref, own_ref, other_ref, out_ref, packed, work, panel, *, count):
    half = own_ref.shape[0]
    core = core_ref[0]
    packed[pl.ds(pl.multiple_of(core * half, half), half), :] = own_ref[...]
    packed[pl.ds(pl.multiple_of((1 - core) * half, half), half), :] = other_ref[...]
    modes = count * LANE
    pairs = tile_pairs(count)
    for t, (i, j) in enumerate(pairs):
        work[LANE * i : LANE * i + LANE, LANE * j : LANE * j + LANE] = packed[LANE * t : LANE * t + LANE, :]
    for i in range(count):
        at = LANE * len(pairs) + 8 * i
        r = jnp.broadcast_to(packed[at : at + 1, :] + packed[at + 1 : at + 2, :], (LANE, LANE))
        work[LANE * i : LANE * i + LANE, modes : modes + LANE] = r.T
    for k in range(count):
        lo = LANE * k
        end = lo + LANE
        x = exact_dot(inverse_block(work[lo:end, lo:end]), work[lo:end, end:])
        panel[lo:end, end:] = x
        for i in range(k + 1, count):
            a = LANE * i
            work[a : a + LANE, a:] -= exact_dot(work[lo:end, a : a + LANE], x[:, a - end :], ((0,), (0,)))
    solved = {}
    for k in reversed(range(count)):
        lo = LANE * k
        u = panel[lo : lo + LANE, modes:]
        for i in range(k + 1, count):
            u = u - exact_dot(panel[lo : lo + LANE, LANE * i : LANE * i + LANE], solved[i])
        solved[k] = u
        out_ref[0:1, lo : lo + LANE] = -u.T[0:1]


def solve_update(core, own, other, modes):
    vmem = pl.BlockSpec(memory_space=pltpu.VMEM)
    return pl.pallas_call(
        functools.partial(solve_kernel, count=modes // LANE),
        out_shape=jax.ShapeDtypeStruct((1, modes), F32),
        in_specs=[pl.BlockSpec(memory_space=pltpu.SMEM), vmem, vmem],
        out_specs=vmem,
        scratch_shapes=[
            pltpu.VMEM((2 * own.shape[0], LANE), F32),
            pltpu.VMEM((modes, modes + LANE), F32),
            pltpu.VMEM((modes, modes + LANE), F32),
        ],
        compiler_params=pltpu.CompilerParams(vmem_limit_bytes=48 * 2**20),
    )(core, own, other)


def swapped(shard):
    return lax.ppermute(shard, CORE, [(0, 1), (1, 0)])


def summed_over_plane(shard, low_rows):
    count = lax.axis_size(PLANE)
    rounded = shard.astype(BF16)
    left_over = jnp.roll(shard - rounded.astype(F32), 1, axis=0).astype(BF16)
    sent = jnp.where(low_rows, left_over, rounded)
    blocks = sent.reshape(count, shard.shape[0] // count, shard.shape[1])
    mine = jnp.sum(lax.all_to_all(blocks, PLANE, 0, 0, tiled=True).astype(F32), axis=0)
    copies = jnp.broadcast_to(mine, blocks.shape)
    return lax.all_to_all(copies, PLANE, 0, 0, tiled=True).reshape(shard.shape)


def edge_kernel(
    nu_ref, adv_ref, rate_ref, first_ref, last_ref, ref_first, ref_last, up_ref, down_ref, rates_ref
):
    modes = first_ref.shape[2]
    for v in range(2):
        up_ref[v : v + 1, :modes] = last_ref[v].astype(F32)[15:16]
        down_ref[v : v + 1, :modes] = first_ref[v].astype(F32)[0:1]
    up_ref[:, modes:] = jnp.broadcast_to(ref_last[:, LANE - 1 : LANE], (2, LANE))
    down_ref[:, modes:] = jnp.broadcast_to(ref_first[:, 0:1], (2, LANE))
    for i, scalar_ref in enumerate((nu_ref, adv_ref, rate_ref)):
        rates_ref[i : i + 1, :] = jnp.full((1, LANE), scalar_ref[0], F32)


def edge_messages(basis, ref, nu, adv, rate):
    cells, modes = basis.shape[1:]
    smem = pl.BlockSpec(memory_space=pltpu.SMEM)

    def whole(shape):
        return pl.BlockSpec(shape, lambda i: (0,) * len(shape))

    shapes = [(2, modes + LANE), (2, modes + LANE), (8, LANE)]
    return pl.pallas_call(
        edge_kernel,
        grid=(1,),
        in_specs=[
            smem, smem, smem,
            pl.BlockSpec((2, 16, modes), lambda i: (0, 0, 0)),
            pl.BlockSpec((2, 16, modes), lambda i: (0, cells // 16 - 1, 0)),
            pl.BlockSpec((2, LANE), lambda i: (0, 0)),
            pl.BlockSpec((2, LANE), lambda i: (0, cells // LANE - 1)),
        ],
        out_specs=[whole(shape) for shape in shapes],
        out_shape=[jax.ShapeDtypeStruct(shape, F32) for shape in shapes],
        compiler_params=pltpu.CompilerParams(vmem_limit_bytes=60 * 2**20),
    )(nu, adv, rate, basis, basis, ref, ref)


def on_device(
    basis_rows,
    reference_state,
    burning,
    coords_now,
    coords_before,
    diffusivity,
    advection,
    reaction_rate,
):
    modes = basis_rows.shape[2]
    size = lax.axis_size(SPACE)
    core = lax.axis_index(CORE).reshape(1)
    up = [(i, i + 1) for i in range(size - 1)]
    up_row, down_row, rates = edge_messages(basis_rows, reference_state, diffusivity, advection, reaction_rate)
    halo_low = lax.ppermute(up_row, SPACE, up)
    halo_high = lax.ppermute(down_row, SPACE, [(j, i) for i, j in up])
    jacobian, residual, own, other = rows_and_sums(
        core, rates, basis_rows, halo_low, halo_high, reference_state, burning[None], coords_now, coords_before
    )
    row = core * own.shape[0] + jnp.arange(own.shape[0], dtype=jnp.int32)
    begin = LANE * len(tile_pairs(modes // LANE))
    low_rows = ((row >= begin) & (row % 8 == 1))[:, None]
    half = summed_over_plane(own + swapped(other), low_rows)
    update = solve_update(core, half, swapped(half), modes)
    return (jacobian[None], residual[None], update)


def solution(mesh):
    split = Mesh(
        mesh.devices.reshape(8, 4, 2, mesh.shape["inst"]), ("space_0", "space_1", "space_2", "inst")
    )
    placed = (
        P(None, SPACE, None),
        P(None, SPACE),
        P(SPACE),
        P("inst", None),
        P("inst", None),
        P("inst"),
        P("inst"),
        P("inst"),
    )
    return jax.shard_map(
        on_device,
        mesh=split,
        in_specs=placed,
        out_specs=(P("inst", None, SPACE, None), P("inst", None, SPACE), P("inst", None)),
        check_vma=False,
    )
```

```python
import functools

import jax
import jax.numpy as jnp
from jax import lax
from jax.experimental import pallas as pl
from jax.experimental.pallas import tpu as pltpu
from jax.sharding import Mesh
from jax.sharding import PartitionSpec as P

PLANE = ("space_0", "space_1")
CORE = "space_2"
SPACE = (*PLANE, CORE)
F32 = jnp.float32
BF16 = jnp.bfloat16

time_step = 0.5
LANE = 128
STEP_CELLS = 768
GRAM_TILES = 2
EXACT = lax.Precision.HIGHEST


def dot_rows(a, b):
    return lax.dot_general(a, b, (((1,), (1,)), ((), ())), preferred_element_type=F32)


def dot_columns(a, b):
    return lax.dot_general(a, b, (((0,), (0,)), ((), ())), preferred_element_type=F32)


def tile_pairs(count):
    return [(i, j) for i in range(count) for j in range(i, count)]


def rows_kernel(*refs, steps, size, edges):
    refs = iter(refs)
    rates_ref, basis_ref, before_ref, after_ref = (next(refs) for _ in range(4))
    ref_ref, burn_ref, now_ref, old_ref = (next(refs) for _ in range(4))
    if edges:
        core_ref, halo_low_ref, halo_high_ref, sums_ref, _, _ = (next(refs) for _ in range(6))
        jac_ref, res_ref, own_ref, other_ref, acc, wide = refs
    else:
        jac_ref, res_ref, acc, wide = refs
    step = pl.program_id(0)
    first, last = step == 0, step == pl.num_programs(0) - 1
    chunk = step * (steps - 1) if edges else step + 1
    modes = basis_ref.shape[2]
    tiles = modes // LANE
    nu, adv, rate = (rates_ref[i : i + 1, 0:1] for i in range(3))
    nu_row, adv_row = rates_ref[0:1, :], rates_ref[1:2, :]
    now = now_ref[...].astype(BF16)
    diff = (now_ref[...] - old_ref[...]).astype(BF16)
    now32 = now.astype(F32)
    coords = jnp.concatenate([now, diff, jnp.zeros((6, modes), BF16)], axis=0)
    start = pl.multiple_of(chunk * size, size)
    lanes = lax.broadcasted_iota(jnp.int32, (1, size), 1)
    state, moved, flux = [], [], []
    for v in range(2):
        low = before_ref[v, 15:16, :].astype(F32)
        high = after_ref[v, 0:1, :].astype(F32)
        below = pl.multiple_of(jnp.maximum(start - LANE, 0), LANE)
        above = pl.multiple_of(jnp.minimum(start + size, (steps - 1) * size), LANE)
        ref_low = ref_ref[v : v + 1, pl.ds(below, LANE)][:, LANE - 1 : LANE]
        ref_high = ref_ref[v : v + 1, pl.ds(above, LANE)][:, 0:1]
        if edges:
            low = jnp.where(first, halo_low_ref[v : v + 1, :modes], low)
            high = jnp.where(last, halo_high_ref[v : v + 1, :modes], high)
            ref_low = jnp.where(first, halo_low_ref[v : v + 1, modes : modes + 1], ref_low)
            ref_high = jnp.where(last, halo_high_ref[v : v + 1, modes : modes + 1], ref_high)
        for m in range(tiles):
            cols = slice(LANE * m, LANE * m + LANE)
            wide[v * tiles + m, 8 : 8 + size, :] = basis_ref[v, :, cols].astype(F32)
            wide[v * tiles + m, 7:8, :] = low[:, cols]
            wide[v * tiles + m, 8 + size : 9 + size, :] = high[:, cols]
        both = dot_rows(coords, basis_ref[v])
        here = ref_ref[v : v + 1, pl.ds(start, size)] + both[0:1]
        state_low = ref_low + jnp.sum(low * now32, axis=1, keepdims=True)
        state_high = ref_high + jnp.sum(high * now32, axis=1, keepdims=True)
        left = jnp.where(lanes == 0, state_low, pltpu.roll(here, 1, 1))
        following = jnp.where(lanes == size - 1, state_high, pltpu.roll(here, size - 1, 1))
        flux.append(nu * (left - 2.0 * here + following) - adv * (here - left))
        state.append(here)
        moved.append(both[1:2])
    active = burn_ref[0:1, pl.ds(start, size)].astype(F32)
    tangent = jnp.tanh(state[1])
    a = rate * active * (1.0 + tangent)
    w = a * state[0]
    e = rate * active * state[0] * (1.0 - tangent * tangent)
    res = [moved[0] - time_step * (flux[0] - w), moved[1] - time_step * (flux[1] + w)]
    res_ref[0:1, :] = res[0]
    res_ref[1:2, :] = res[1]
    mid = 1.0 + time_step * (2.0 * nu_row + adv_row)
    lower = time_step * (nu_row + adv_row)
    upper = time_step * nu_row

    def sides(k, lo):
        return lower * wide[k, 7 + lo : 7 + lo + LANE, :] + upper * wide[k, 9 + lo : 9 + lo + LANE, :]

    half = modes // 2

    @pl.when(first)
    def _():
        if edges:
            acc[0:half, :] = sums_ref[0:half, :]
            acc[half:, half:] = sums_ref[half:, half:]
            acc[modes:, :half] = sums_ref[modes:, :half]
        else:
            acc[...] = jnp.zeros_like(acc)

    rounded = [jnp.broadcast_to(x.astype(BF16), (8, size)) for x in res]
    for t in range(size // LANE):
        lo = LANE * t
        a_col = jnp.broadcast_to(time_step * a[:, lo : lo + LANE], (LANE, LANE)).T
        e_col = jnp.broadcast_to(time_step * e[:, lo : lo + LANE], (LANE, LANE)).T
        fuel_own = mid + a_col
        heat_own = mid - e_col
        for m in range(tiles):
            cols = slice(LANE * m, LANE * m + LANE)
            p = wide[m, 8 + lo : 8 + lo + LANE, :]
            q = wide[tiles + m, 8 + lo : 8 + lo + LANE, :]
            fuel = fuel_own * p + e_col * q - sides(m, lo)
            heat = heat_own * q - a_col * p - sides(tiles + m, lo)
            jac_ref[0, lo : lo + LANE, cols] = fuel.astype(BF16)
            jac_ref[1, lo : lo + LANE, cols] = heat.astype(BF16)
        if (t + 1) % GRAM_TILES == 0:
            span = slice(lo + LANE - GRAM_TILES * LANE, lo + LANE)
            j = jnp.concatenate([jac_ref[0, span, :], jac_ref[1, span, :]], axis=0)
            both_res = jnp.concatenate([x[:, span] for x in rounded], axis=1)
            acc[modes:, :] += jnp.dot(both_res, j, preferred_element_type=F32)
            acc[0:half, :] += dot_columns(j[:, :half], j)
            acc[half:modes, half:] += dot_columns(j[:, half:], j[:, half:])

    if not edges:
        return

    def write(target, which):
        pairs = tile_pairs(modes // LANE)
        rows_half = target.shape[0]
        base = which * rows_half
        for t, (i, j) in enumerate(pairs):
            at = LANE * t - base
            if 0 <= at < rows_half:
                target[at : at + LANE, :] = acc[LANE * i : LANE * i + LANE, LANE * j : LANE * j + LANE]
        at = LANE * len(pairs) - base
        if 0 <= at < rows_half:
            target[at:, :] = jnp.zeros((rows_half - at, LANE), F32)
            for i in range(modes // LANE):
                target[at + 8 * i : at + 8 * i + 1, :] = acc[modes : modes + 1, LANE * i : LANE * i + LANE]

    for core in range(2):

        @pl.when(last & (core_ref[0] == core))
        def _():
            write(own_ref, core)
            write(other_ref, 1 - core)


def packed_rows(modes):
    count = modes // LANE
    return -(-(LANE * len(tile_pairs(count)) + 8 * count) // 512) * 512


def rows_call(rates, basis, ref, burn, now, old, edge_args=None):
    cells, modes = basis.shape[1:]
    size = STEP_CELLS
    steps = cells // size
    per = size // 16
    edges = edge_args is not None
    smem = pl.BlockSpec(memory_space=pltpu.SMEM)
    half = packed_rows(modes) // 2

    def chunk(i):
        return i * (steps - 1) if edges else i + 1

    def whole(shape):
        return pl.BlockSpec(shape, lambda i: (0,) * len(shape))

    in_specs = [
        whole(rates.shape),
        pl.BlockSpec((2, size, modes), lambda i: (0, chunk(i), 0)),
        pl.BlockSpec((2, 16, modes), lambda i: (0, jnp.maximum(chunk(i) * per - 1, 0), 0)),
        pl.BlockSpec((2, 16, modes), lambda i: (0, jnp.minimum(chunk(i) * per + per, cells // 16 - 1), 0)),
        whole(ref.shape), whole(burn.shape), whole(now.shape), whole(old.shape),
    ]
    out_specs = [
        pl.BlockSpec((2, size, modes), lambda i: (0, chunk(i), 0)),
        pl.BlockSpec((2, size), lambda i: (0, chunk(i))),
    ]
    out_shape = [
        jax.ShapeDtypeStruct((2, cells, modes), BF16),
        jax.ShapeDtypeStruct((2, cells), F32),
    ]
    sums_shape = [jax.ShapeDtypeStruct((modes + 8, modes), F32)]
    scratch = [pltpu.VMEM((2 * (modes // LANE), size + 16, LANE), F32)]
    args = [rates, basis, basis, basis, ref, burn, now, old]
    aliases = {}
    if edges:
        anywhere = pl.BlockSpec(memory_space=pl.ANY)
        args += edge_args
        in_specs += [smem] + [whole(a.shape) for a in edge_args[1:4]] + [anywhere, anywhere]
        out_specs += [whole((half, LANE))] * 2
        out_shape += [jax.ShapeDtypeStruct((half, LANE), F32)] * 2
        scratch = [pltpu.VMEM(s.shape, s.dtype) for s in sums_shape] + scratch
        aliases = {len(args) - 2: 0, len(args) - 1: 1}
    else:
        out_specs += [whole(s.shape) for s in sums_shape]
        out_shape += sums_shape
    return pl.pallas_call(
        functools.partial(rows_kernel, steps=steps, size=size, edges=edges),
        grid=(2 if edges else steps - 2,),
        in_specs=in_specs,
        out_specs=out_specs,
        out_shape=out_shape,
        scratch_shapes=scratch,
        input_output_aliases=aliases,
        compiler_params=pltpu.CompilerParams(vmem_limit_bytes=(48 if edges else 60) * 2**20),
    )(*args)


def rows_and_sums(core, rates, basis, halo_low, halo_high, ref, burn, now, old):
    common = (rates, basis, ref, burn, now, old)
    jacobian, residual, sums = rows_call(*common)
    return rows_call(*common, [core, halo_low, halo_high, sums, jacobian, residual])


def reciprocal(x):
    return pltpu.reciprocal(x, approx=True)


def inverse_block(block):
    width = block.shape[1]
    groups = [block[8 * g : 8 * g + 8] for g in range(width // 8)]
    full = (8, width)
    lanes = lax.broadcasted_iota(jnp.int32, full, 1)
    subs = lax.broadcasted_iota(jnp.int32, full, 0)
    for p in range(len(groups)):
        panel = groups[p]
        base = 8 * p
        cols = [jnp.broadcast_to(panel[:, base + j : base + j + 1], full) for j in range(8)]
        window = (lanes >= base) & (lanes < base + 8)
        opened = jnp.where(window, jnp.where(lanes == subs + base, 1.0, 0.0), panel)
        scale = jnp.zeros(full, F32)
        for j in range(8):
            inv = reciprocal(jnp.broadcast_to(cols[j][j : j + 1], full))
            mult = jnp.where(subs == j, 0.0, cols[j]) * inv
            scale = jnp.where(subs == j, inv, scale)
            for t in range(j + 1, 8):
                cols[t] = cols[t] - mult * jnp.broadcast_to(cols[t][j : j + 1], full)
            opened = opened - mult * jnp.broadcast_to(opened[j : j + 1], full)
        whole = opened * scale
        rows = [jnp.broadcast_to(whole[s : s + 1], full) for s in range(8)]
        order = [*range(p + 1, len(groups)), *range(p)]
        for g in order:
            terms = [jnp.broadcast_to(groups[g][:, base + s : base + s + 1], full) * rows[s] for s in range(8)]
            while len(terms) > 1:
                terms = [a + b for a, b in zip(terms[::2], terms[1::2])]
            groups[g] = jnp.where(window, 0.0, groups[g]) - terms[0]
        groups[p] = whole
    return jnp.concatenate(groups, axis=0)


def exact_dot(a, b, dims=((1,), (0,))):
    return lax.dot_general(a, b, (dims, ((), ())), precision=EXACT, preferred_element_type=F32)


def solve_kernel(core_ref, own_ref, other_ref, out_ref, packed, work, panel, *, count):
    half = own_ref.shape[0]
    core = core_ref[0]
    packed[pl.ds(pl.multiple_of(core * half, half), half), :] = own_ref[...]
    packed[pl.ds(pl.multiple_of((1 - core) * half, half), half), :] = other_ref[...]
    modes = count * LANE
    pairs = tile_pairs(count)
    for t, (i, j) in enumerate(pairs):
        work[LANE * i : LANE * i + LANE, LANE * j : LANE * j + LANE] = packed[LANE * t : LANE * t + LANE, :]
    for i in range(count):
        at = LANE * len(pairs) + 8 * i
        r = jnp.broadcast_to(packed[at : at + 1, :] + packed[at + 1 : at + 2, :], (LANE, LANE))
        work[LANE * i : LANE * i + LANE, modes : modes + LANE] = r.T
    for k in range(count):
        lo = LANE * k
        end = lo + LANE
        x = exact_dot(inverse_block(work[lo:end, lo:end]), work[lo:end, end:])
        panel[lo:end, end:] = x
        for i in range(k + 1, count):
            a = LANE * i
            work[a : a + LANE, a:] -= exact_dot(work[lo:end, a : a + LANE], x[:, a - end :], ((0,), (0,)))
    solved = {}
    for k in reversed(range(count)):
        lo = LANE * k
        u = panel[lo : lo + LANE, modes:]
        for i in range(k + 1, count):
            u = u - exact_dot(panel[lo : lo + LANE, LANE * i : LANE * i + LANE], solved[i])
        solved[k] = u
        out_ref[0:1, lo : lo + LANE] = -u.T[0:1]


def solve_update(core, own, other, modes):
    vmem = pl.BlockSpec(memory_space=pltpu.VMEM)
    return pl.pallas_call(
        functools.partial(solve_kernel, count=modes // LANE),
        out_shape=jax.ShapeDtypeStruct((1, modes), F32),
        in_specs=[pl.BlockSpec(memory_space=pltpu.SMEM), vmem, vmem],
        out_specs=vmem,
        scratch_shapes=[
            pltpu.VMEM((2 * own.shape[0], LANE), F32),
            pltpu.VMEM((modes, modes + LANE), F32),
            pltpu.VMEM((modes, modes + LANE), F32),
        ],
        compiler_params=pltpu.CompilerParams(vmem_limit_bytes=48 * 2**20),
    )(core, own, other)


def swapped(shard):
    return lax.ppermute(shard, CORE, [(0, 1), (1, 0)])


def summed_over_plane(shard, low_rows):
    count = lax.axis_size(PLANE)
    rounded = shard.astype(BF16)
    left_over = jnp.roll(shard - rounded.astype(F32), 1, axis=0).astype(BF16)
    sent = jnp.where(low_rows, left_over, rounded)
    blocks = sent.reshape(count, shard.shape[0] // count, shard.shape[1])
    mine = jnp.sum(lax.all_to_all(blocks, PLANE, 0, 0, tiled=True).astype(F32), axis=0)
    copies = jnp.broadcast_to(mine, blocks.shape)
    return lax.all_to_all(copies, PLANE, 0, 0, tiled=True).reshape(shard.shape)


def edge_kernel(
    nu_ref, adv_ref, rate_ref, first_ref, last_ref, ref_first, ref_last, up_ref, down_ref, rates_ref
):
    modes = first_ref.shape[2]
    for v in range(2):
        up_ref[v : v + 1, :modes] = last_ref[v].astype(F32)[15:16]
        down_ref[v : v + 1, :modes] = first_ref[v].astype(F32)[0:1]
    up_ref[:, modes:] = jnp.broadcast_to(ref_last[:, LANE - 1 : LANE], (2, LANE))
    down_ref[:, modes:] = jnp.broadcast_to(ref_first[:, 0:1], (2, LANE))
    for i, scalar_ref in enumerate((nu_ref, adv_ref, rate_ref)):
        rates_ref[i : i + 1, :] = jnp.full((1, LANE), scalar_ref[0], F32)


def edge_messages(basis, ref, nu, adv, rate):
    cells, modes = basis.shape[1:]
    smem = pl.BlockSpec(memory_space=pltpu.SMEM)

    def whole(shape):
        return pl.BlockSpec(shape, lambda i: (0,) * len(shape))

    shapes = [(2, modes + LANE), (2, modes + LANE), (8, LANE)]
    return pl.pallas_call(
        edge_kernel,
        grid=(1,),
        in_specs=[
            smem, smem, smem,
            pl.BlockSpec((2, 16, modes), lambda i: (0, 0, 0)),
            pl.BlockSpec((2, 16, modes), lambda i: (0, cells // 16 - 1, 0)),
            pl.BlockSpec((2, LANE), lambda i: (0, 0)),
            pl.BlockSpec((2, LANE), lambda i: (0, cells // LANE - 1)),
        ],
        out_specs=[whole(shape) for shape in shapes],
        out_shape=[jax.ShapeDtypeStruct(shape, F32) for shape in shapes],
        compiler_params=pltpu.CompilerParams(vmem_limit_bytes=60 * 2**20),
    )(nu, adv, rate, basis, basis, ref, ref)


def on_device(
    basis_rows,
    reference_state,
    burning,
    coords_now,
    coords_before,
    diffusivity,
    advection,
    reaction_rate,
):
    modes = basis_rows.shape[2]
    size = lax.axis_size(SPACE)
    core = lax.axis_index(CORE).reshape(1)
    up = [(i, i + 1) for i in range(size - 1)]
    up_row, down_row, rates = edge_messages(basis_rows, reference_state, diffusivity, advection, reaction_rate)
    halo_low = lax.ppermute(up_row, SPACE, up)
    halo_high = lax.ppermute(down_row, SPACE, [(j, i) for i, j in up])
    jacobian, residual, own, other = rows_and_sums(
        core, rates, basis_rows, halo_low, halo_high, reference_state, burning[None], coords_now, coords_before
    )
    row = core * own.shape[0] + jnp.arange(own.shape[0], dtype=jnp.int32)
    begin = LANE * len(tile_pairs(modes // LANE))
    low_rows = ((row >= begin) & (row % 8 == 1))[:, None]
    half = summed_over_plane(own + swapped(other), low_rows)
    update = solve_update(core, half, swapped(half), modes)
    return (jacobian[None], residual[None], update)


def solution(mesh):
    split = Mesh(
        mesh.devices.reshape(8, 4, 2, mesh.shape["inst"]), ("space_0", "space_1", "space_2", "inst")
    )
    placed = (
        P(None, SPACE, None),
        P(None, SPACE),
        P(SPACE),
        P("inst", None),
        P("inst", None),
        P("inst"),
        P("inst"),
        P("inst"),
    )
    return jax.shard_map(
        on_device,
        mesh=split,
        in_specs=placed,
        out_specs=(P("inst", None, SPACE, None), P("inst", None, SPACE), P("inst", None)),
        check_vma=False,
    )
```
